512 devices in a mesh: row: 32 (over z, y_lo), col: 16 (over x, y_hi, core).
Axes of the slice: x: 4, y: 4 (y_hi: 2, y_lo: 2; y = y_hi * 2 + y_lo), z: 16, core: 2. Of those that a mesh axis runs over, the one named last changes fastest.
Arguments:
- valence: bfloat16 [512, 373248], P(('row', 'col')), may hold values from -6 to 6
- conduction: bfloat16 [512, 373248], P(('row', 'col')), may hold values from -6 to 6
- val_energy: float32 [512], replicated, may hold values from -14 to -2
- cond_energy: float32 [512], P(('row', 'col')), may hold values from 0.5 to 24
- owner: int32 [2], replicated, may hold values from 0 to 511
- g_index: int32 [8192], replicated, may hold values from 0 to 373247, as said below
Outputs:
- chi_zero: float32 [8192, 8192], P('row', 'col')
The draws below stay inside these ranges and needn't reach their ends.
Inputs may be any that keep to these rules, and one draw needn't show every extreme that they name: `g_index`: distinct flat indices (i * 72 + j) * 72 + k. Taking each of i, j, k into -36 .. 35, each of them lies in -18 .. 17, and they are the 8192 frequency vectors of smallest squared length, listed in non-decreasing squared length; within a shell, and in the partly taken outermost shell, the choice and order come from the seed.
All inputs are finite; a program needn't handle non-finite values.
Results may differ from the reference program's by a relative error of at most 0.0038.
Values may be sent and summed in bfloat16 or wider, within the bound.
No kernel may reach another device: no remote copies, remote signals or barrier semaphores. Data moves between devices by JAX's collectives and lax.ppermute only.
A program may use at most 128 MiB of HBM per device.

```python
import math
import jax
import jax.numpy as jnp
from jax import lax

GRID = 72
NG = 8192
VSTEPS = 2
CB = 512
VALENCE = 512


def draw_g_index(key, part):
    key = jax.random.fold_in(key, 7)
    half = GRID // 4
    side = 2 * half
    count = side ** 3
    cells = jnp.arange(count, dtype=jnp.int32)
    first = cells // (side * side) - half
    second = cells // side % side - half
    third = cells % side - half
    length = first * first + second * second + third * third
    ties = jax.random.permutation(key, count).astype(jnp.int32)
    score = length * count + ties
    _, picked = lax.top_k(-score, NG)
    first = first[picked] % GRID
    second = second[picked] % GRID
    third = third[picked] % GRID
    return ((first * GRID + second) * GRID + third).astype(jnp.int32)


def level_of(own_key, dims, split, least, largest):
    def one(position, shards_of):
        heights = jax.random.uniform(jax.random.fold_in(jax.random.fold_in(own_key, 6), position), (shards_of,), jnp.float32, least / len(split), largest / len(split))
        return jnp.repeat(jnp.exp(heights), dims[position] // shards_of).reshape((-1,) + (1,) * (len(dims) - position - 1))

    gain = one(*split[0])
    for cut in split[1:]:
        gain = gain * one(*cut)
    return gain


def scatter_about(rng, shape, deviation, reach, split=(), held_as=jnp.bfloat16):
    factor_of = level_of(rng, shape, split, -0.22, 0.18) if split else 1.0
    drawn = jax.random.normal(rng, shape, jnp.float32) * deviation * factor_of
    return jnp.minimum(jnp.maximum(drawn, -reach), reach).astype(held_as)


def setup_inputs(seed: int = 0) -> dict:
    key_list = jax.random.split(jax.random.key(seed), 7)
    valence = scatter_about(key_list[0], (VALENCE, GRID * GRID * GRID), 1.0, 6.0, ((0, 512),))
    conduction = scatter_about(key_list[1], (CB, GRID * GRID * GRID), 1.0, 6.0, ((0, 512),))
    val_energy = jnp.clip(jax.random.uniform(key_list[2], (VALENCE,), jnp.float32, -14.0, -2.0), -14.0, -2.0)
    cond_energy = jnp.clip(0.5 + 23.5 * jax.random.uniform(key_list[3], (CB,), jnp.float32) ** level_of(key_list[3], (CB,), ((0, 512),), -0.2, 0.2), 0.5, 24.0)
    owner = jax.random.randint(key_list[4], (VSTEPS,), 0, VALENCE).astype(jnp.int32)
    g_index = draw_g_index(jax.random.fold_in(key_list[6], 71), 0)
    return {"valence": valence, "conduction": conduction, "val_energy": val_energy, "cond_energy": cond_energy, "owner": owner, "g_index": g_index}


def reference(valence, conduction, val_energy, cond_energy, owner, g_index):
    total = jnp.zeros((NG, NG), jnp.float32)
    for step in range(VSTEPS):
        band = owner[step]
        psi_v = lax.dynamic_index_in_dim(valence, band, 0, keepdims=False).astype(jnp.float32)
        e_v = val_energy[band]

        def pair(args):
            psi_c, e_c = args
            rho = psi_v * psi_c.astype(jnp.float32)
            spec = jnp.fft.fftn(rho.reshape(GRID, GRID, GRID)).reshape(-1)[g_index]
            scale = jnp.sqrt(4.0 / (e_c - e_v)) / math.sqrt(GRID ** 3)
            return jnp.stack([jnp.real(spec) * scale, jnp.imag(spec) * scale]).astype(jnp.bfloat16)
        elems = lax.map(pair, (conduction, cond_energy))
        flat = elems.reshape(2 * CB, NG).astype(jnp.float32)
        total = total + jnp.dot(flat.T, flat, precision=lax.Precision.HIGHEST)
    return -total / math.sqrt(VSTEPS * CB)
```

```python
import math

import jax
import jax.numpy as jnp
from jax import lax
from jax.sharding import Mesh, PartitionSpec as P

GRID = 72
VSTEPS = 2
AXES = ("z", "yl", "x", "yh", "c")
SIZES = (16, 2, 4, 2, 2)
ROW = ("z", "yl")
COL = ("x", "yh", "c")
PLANE = ("yl", "x", "yh", "c")
TILE = ("yl", "x", "yh")
LANES = 128
PIECE = 6
CHUNK = 16 * PIECE


def exchange(x, axis):
    return lax.all_to_all(x, axis, split_axis=0, concat_axis=0, tiled=True)


def from_owners(shard, owner):
    size = shard.shape[1]
    steps = owner.shape[0]
    owner_z, owner_plane = owner // 32, owner % 32
    flat = jnp.pad(shard.reshape(size // LANES, LANES), ((0, 32 * CHUNK - size // LANES), (0, 0)))
    parts = exchange(flat.reshape(32, CHUNK, LANES), PLANE)
    parts = jnp.stack([lax.dynamic_index_in_dim(parts, owner_plane[s], 0, False) for s in range(steps)])
    parts = parts.reshape(steps, 16, PIECE, LANES).transpose(1, 0, 2, 3)
    parts = exchange(parts, "z")
    parts = jnp.stack([lax.dynamic_index_in_dim(parts[:, s], owner_z[s], 0, False) for s in range(steps)])
    parts = exchange(jnp.broadcast_to(parts[None], (16,) + parts.shape), "z")
    parts = parts.transpose(1, 0, 2, 3).reshape(steps * CHUNK, LANES)
    parts = exchange(jnp.broadcast_to(parts[None], (16,) + parts.shape), TILE)
    other = lax.ppermute(parts, "c", [(0, 1), (1, 0)])
    first = lax.axis_index("c") == 0
    both = jnp.stack([jnp.where(first, parts, other), jnp.where(first, other, parts)], axis=1)
    both = both.reshape(32, steps, CHUNK, LANES).transpose(1, 0, 2, 3)
    return both.reshape(steps, 32 * CHUNK, LANES)


def make_tables(size, quarter):
    inputs = jnp.arange(size, dtype=jnp.int32)
    wanted = (jnp.arange(2 * quarter, dtype=jnp.int32) - quarter) % size
    phase = inputs[:, None] * wanted[None, :] % size
    angle = phase.astype(jnp.float32) * (2.0 * math.pi / size)
    back_table = jnp.concatenate([jnp.cos(angle), -jnp.sin(angle)], axis=1)
    return (back_table.T, back_table)


def combine(mixed, width):
    real_part = mixed[0, ..., :width, :] - mixed[1, ..., width:, :]
    imag_part = mixed[0, ..., width:, :] + mixed[1, ..., :width, :]
    return jnp.stack([real_part, imag_part])


def spectrum(rho, front_table, back_table, size, width):
    highest = lax.Precision.HIGHEST
    first = jnp.dot(front_table, rho.reshape(size, size * size), precision=highest)
    first = first.reshape(2, width, size, size)
    second = jnp.einsum("wj,pmjk->pmwk", front_table, first, precision=highest)
    second = combine(second, width)
    third = jnp.dot(second.reshape(2 * width * width, size), back_table, precision=highest)
    third = third.reshape(2, width * width, 2 * width)
    real_part = third[0, :, :width] - third[1, :, width:]
    imag_part = third[0, :, width:] + third[1, :, :width]
    return jnp.stack([real_part.reshape(-1), imag_part.reshape(-1)])


def body(valence, conduction, val_energy, cond_energy, owner, g_index):
    size = GRID
    quarter = size // 4
    width = 2 * quarter
    front_table, back_table = make_tables(size, quarter)
    first_pos = (g_index // (size * size) + quarter) % size
    second_pos = (g_index // size % size + quarter) % size
    third_pos = (g_index % size + quarter) % size
    flat_at = (first_pos * width + second_pos) * width + third_pos
    bands_here = conduction.shape[0]
    nrow = lax.axis_size(ROW)
    ncol = lax.axis_size(COL)
    psi = from_owners(valence, owner)[:, : size**3 // LANES]
    total = jnp.zeros((g_index.shape[0] // nrow, g_index.shape[0] // ncol), jnp.float32)
    for step in range(VSTEPS):
        psi_v = psi[step].reshape(-1)
        pair_psi_v = psi_v
        pair_psi_v = pair_psi_v.astype(jnp.float32)
        rows_out = []
        rho = pair_psi_v * conduction[0].astype(jnp.float32)
        parts = spectrum(rho, front_table, back_table, size, width)
        scale = jnp.sqrt(4.0 / (cond_energy[0] - val_energy[owner[step]])) / math.sqrt(size**3)
        picked = jnp.take(parts, flat_at, axis=1) * scale
        rows_out.append(picked[0])
        rows_out.append(picked[1])
        elems = jnp.stack(rows_out).astype(jnp.bfloat16)
        count = elems.shape[0]
        rows_side = lax.all_to_all(elems, ROW, split_axis=1, concat_axis=0, tiled=True)
        cols_side = lax.all_to_all(elems, COL, split_axis=1, concat_axis=0, tiled=True)
        rows_side = rows_side.reshape(1, nrow, count, rows_side.shape[1])
        cols_side = cols_side.reshape(1, ncol, count, cols_side.shape[1])
        whole = lax.all_gather(cols_side, ROW, axis=0, tiled=True)
        total = total + jnp.einsum(
            "crlg,rclh->gh",
            lax.all_gather(rows_side, COL, axis=0, tiled=True),
            whole,
            preferred_element_type=jnp.float32,
        )
    bands_all = VSTEPS * bands_here * nrow * ncol
    return -total / math.sqrt(bands_all)


def solution(mesh):
    every = P(AXES)
    return jax.shard_map(
        body,
        mesh=Mesh(mesh.devices.reshape(SIZES), AXES),
        in_specs=(P(AXES, None), P(AXES, None), P(), every, P(), P()),
        out_specs=P(ROW, COL),
        check_vma=False,
    )
```

```python
import math

import jax
import jax.numpy as jnp
import ml_dtypes
import numpy as np
from jax import lax
from jax.experimental import pallas as pl
from jax.experimental.pallas import tpu as pltpu
from jax.sharding import Mesh, PartitionSpec as P

GRID = 72
STEPS = 2
AXES = ("z", "yl", "x", "yh", "c")
SIZES = (16, 2, 4, 2, 2)
ROW = ("z", "yl")
COL = ("x", "yh", "c")
PLANE = ("yl", "x", "yh", "c")
TILE = ("yl", "x", "yh")
QUAD = ("x", "yh")
LANES = 128
PIECE = 6
CHUNK = 16 * PIECE
SWAP = [(0, 1), (1, 0)]
REACH=12
KEPT=2*REACH+1
HALF=GRID//2
PAIR=GRID*GRID*2//LANES
ROWS=GRID**3//LANES
WIDE=16
BACK=32
SLOT=64
PAD_ROWS=40*PAIR


def exchange(x, axis):
    return lax.all_to_all(x, axis, split_axis=0, concat_axis=0, tiled=True)


def from_owners(shard, owner):
    size = shard.shape[1]
    steps = owner.shape[0]
    owner_z, owner_plane = owner // 32, owner % 32
    flat = jnp.pad(shard.reshape(size // LANES, LANES), ((0, 32 * CHUNK - size // LANES), (0, 0)))
    parts = exchange(flat.reshape(32, CHUNK, LANES), PLANE)
    parts = jnp.stack([lax.dynamic_index_in_dim(parts, owner_plane[s], 0, False) for s in range(steps)])
    parts = parts.reshape(steps, 16, PIECE, LANES).transpose(1, 0, 2, 3)
    parts = exchange(parts, "z")
    parts = jnp.stack([lax.dynamic_index_in_dim(parts[:, s], owner_z[s], 0, False) for s in range(steps)])
    parts = exchange(jnp.broadcast_to(parts[None], (16,) + parts.shape), "z")
    parts = parts.transpose(1, 0, 2, 3).reshape(steps * CHUNK, LANES)
    parts = exchange(jnp.broadcast_to(parts[None], (16,) + parts.shape), TILE)
    other = lax.ppermute(parts, "c", SWAP)
    first = lax.axis_index("c") == 0
    both = jnp.stack([jnp.where(first, parts, other), jnp.where(first, other, parts)], axis=1)
    both = both.reshape(32, steps, CHUNK, LANES).transpose(1, 0, 2, 3)
    return both.reshape(steps, 32 * CHUNK, LANES)


def split(x):
    high=x.astype(jnp.bfloat16)
    return high,(x-high.astype(jnp.float32)).astype(jnp.bfloat16)

def split_np(x):
    h=x.astype(ml_dtypes.bfloat16)
    return h,(x-h.astype(np.float64)).astype(ml_dtypes.bfloat16)

def tables():
    point=np.arange(GRID)
    def cs(freq):
        ang=2*math.pi*((freq[:,None]*point[None,:])%GRID)/GRID
        return np.cos(ang),np.sin(ang)
    c,s=cs(np.arange(REACH+1))
    t=np.zeros((2,WIDE,2,40))
    t[0,:REACH+1,0,:HALF]=c[:,0::2]; t[0,:REACH+1,1,:HALF]=c[:,1::2]
    t[1,:REACH+1,0,:HALF]=-s[:,0::2]; t[1,:REACH+1,1,:HALF]=-s[:,1::2]
    t=t.reshape(2*WIDE,80)
    h,l=split_np(t)
    first=np.concatenate([h,h,l],1)
    c,s=cs(np.arange(-REACH,REACH+1))
    w=np.zeros((2,LANES,2,SLOT))
    w[0,:GRID,0,:KEPT]=c.T; w[0,:GRID,1,:KEPT]=-s.T
    w[1,:GRID,0,:KEPT]=s.T; w[1,:GRID,1,:KEPT]=c.T
    w=w.reshape(2*LANES,LANES)
    h,l=split_np(w)
    third=np.concatenate([h,l],1)
    u=np.zeros((2,BACK,GRID))
    u[0,:KEPT]=c; u[1,:KEPT]=s
    u=u.reshape(2*BACK,GRID)
    h,l=split_np(u)
    second=np.concatenate([h,h,l],1)
    return first,second,third

def dft_kernel(scale, psi, cond, first, second, third, place, lane, sign, out, vals, held, mixed, spread):
    f32=jnp.float32; bf=jnp.bfloat16
    tail=PAD_ROWS-ROWS
    for s in range(STEPS):
        vals[s,:ROWS,:]=psi[s,:ROWS,:].astype(f32)*cond[:ROWS,:].astype(f32)
        vals[s,ROWS:,:]=jnp.zeros((tail,LANES),f32)
    left=lax.broadcasted_iota(jnp.int32,(40,LANES),1)<LANES//2
    table=first[...]
    zero=jnp.zeros((40,LANES),f32)
    rolled=[pltpu.roll(vals[s,pl.ds(40,40,stride=PAIR),:],LANES//2,1) for s in range(STEPS)]
    for t in range(41):
        cols=[]
        for s in range(STEPS):
            even=vals[s,pl.ds(t,40,stride=PAIR),:]
            here=rolled[s]
            ahead=pltpu.roll(vals[s,pl.ds(41+t,40,stride=PAIR),:],LANES//2,1) if t<40 else zero
            rolled[s]=ahead
            odd=jnp.where(left,here,ahead)
            x=jnp.concatenate([even,odd],0)
            h=x.astype(bf).astype(f32)
            cols.append(jnp.concatenate([h,x-h,h],0).astype(bf))
        y=jnp.dot(table,jnp.concatenate(cols,1),preferred_element_type=f32)
        for s in range(STEPS):
            held[s,:,t*LANES:(t+1)*LANES]=y[:,s*LANES:(s+1)*LANES]
    w=third[...]
    group=8
    for j0 in range(0,GRID,group):
        parts=[[],[]]
        for j in range(j0,j0+group):
            for s in range(STEPS):
                x=held[s,:,j*GRID:j*GRID+LANES]
                parts[0].append(x[:WIDE]); parts[1].append(x[WIDE:])
        x=jnp.concatenate([jnp.concatenate(parts[0],0),jnp.concatenate(parts[1],0)],1)
        h,l=split(x)
        y=jnp.dot(h,w,preferred_element_type=f32)
        z=jnp.dot(l,w[:,:LANES],preferred_element_type=f32)
        mixed[j0*32:(j0+group)*32,:]=y[:,:LANES]+y[:,LANES:]+z
    table=second[...]
    flip=jnp.where(lax.broadcasted_iota(jnp.int32,(BACK,LANES),1)<SLOT,1.0,-1.0).astype(f32)
    for i in range(REACH+1):
        cols=[]
        for s in range(STEPS):
            x=mixed[pl.ds(s*WIDE+i,GRID,stride=32),:]
            h=x.astype(bf).astype(f32)
            cols.append(jnp.concatenate([h,x-h,h],0).astype(bf))
        y=jnp.dot(table,jnp.concatenate(cols,1),preferred_element_type=f32)
        for s in range(STEPS):
            z=y[:,s*LANES:(s+1)*LANES]
            r=(z[:BACK]+flip*pltpu.roll(z[BACK:],SLOT,1))*scale[s]
            spread[s*LANES:(s+1)*LANES, i*BACK:(i+1)*BACK]=r.T.astype(bf)
    tile=512
    rows=(REACH+1)*BACK
    data=spread[...]
    at=lax.broadcasted_iota(jnp.int32,(rows,tile),0)
    slot=lax.broadcasted_iota(jnp.int32,(SLOT,tile),0)
    def pick(n,_):
        here=pl.ds(pl.multiple_of(n*tile,tile),tile)
        hot=jnp.where(at==place[:,here],1.0,0.0).astype(bf)
        y=jnp.dot(data,hot,preferred_element_type=f32)
        keep=slot==lane[:,here]
        r=[jnp.sum(jnp.where(keep,y[p*SLOT:(p+1)*SLOT],0.0),0,keepdims=True) for p in range(2*STEPS)]
        sg=sign[:,here]
        out[:,here]=jnp.concatenate([r[0],r[1]*sg,r[2],r[3]*sg],0).astype(bf)
        return 0
    lax.fori_loop(0,place.shape[1]//tile,pick,0)

def pairs(psi, cond, scale, g_index):
    third=g_index%GRID; second=g_index//GRID%GRID; first=g_index//(GRID*GRID)
    mid=GRID//2
    i=jnp.where(first<mid,first,first-GRID); j=jnp.where(second<mid,second,second-GRID); k=jnp.where(third<mid,third,third-GRID)
    sg=jnp.where(i<0,-1,1)
    place=i*sg*BACK+(j*sg+REACH)
    lane=k*sg+REACH
    a,b,c=[jnp.asarray(x) for x in tables()]
    ng=g_index.shape[0]
    vm=pl.BlockSpec(memory_space=pltpu.VMEM)
    return pl.pallas_call(dft_kernel,
        out_shape=jax.ShapeDtypeStruct((2*STEPS,ng),jnp.bfloat16),
        in_specs=[pl.BlockSpec(memory_space=pltpu.SMEM)]+[vm]*8,
        out_specs=vm,
        scratch_shapes=[pltpu.VMEM((STEPS,PAD_ROWS,LANES),jnp.float32),
            pltpu.VMEM((STEPS,2*WIDE,41*LANES),jnp.float32),
            pltpu.VMEM((GRID*32,LANES),jnp.float32),
            pltpu.VMEM((STEPS*LANES,(REACH+1)*BACK),jnp.bfloat16)],
        compiler_params=pltpu.CompilerParams(vmem_limit_bytes=48*2**20),
    )(scale,psi,cond,a,b,c,place[None],lane[None],sg.astype(jnp.float32)[None])


def body(valence, conduction, val_energy, cond_energy, owner, g_index):
    bands = STEPS * 512
    psi = from_owners(valence, owner)
    cond = conduction.reshape(ROWS, LANES)
    scale = jnp.sqrt(4.0 / (cond_energy[0] - val_energy[owner])) / math.sqrt(GRID**3)
    elems = pairs(psi, cond, scale, g_index)
    count = elems.shape[0]
    ng = elems.shape[1]
    rows = exchange(elems.reshape(count, 16, ng // 16).transpose(1, 0, 2), "z").transpose(1, 0, 2)
    rows = exchange(jnp.broadcast_to(rows[None], (8,) + rows.shape), QUAD)
    other = lax.ppermute(rows, "c", SWAP)
    first = lax.axis_index("c") == 0
    rows = jnp.stack([jnp.where(first, rows, other), jnp.where(first, other, rows)], axis=1)
    cols = exchange(elems.reshape(count, 16, ng // 16).transpose(1, 0, 2), COL).transpose(1, 0, 2)
    cols = exchange(jnp.broadcast_to(cols[None], (16,) + cols.shape), "z")
    cols = cols.reshape(16, count, 8, 2, ng // 16)
    part = jnp.einsum("mclzg,zlmch->gh", rows, cols, preferred_element_type=jnp.float32)
    part = part.reshape(2, ng // 32, ng // 16)
    mine = lax.axis_index("yl")
    away = lax.dynamic_index_in_dim(part, 1 - mine, 0, False).astype(jnp.bfloat16)
    here = lax.dynamic_index_in_dim(part, mine, 0, False)
    total = here + lax.ppermute(away, "yl", SWAP).astype(jnp.float32)
    return -total / math.sqrt(bands)


def solution(mesh):
    every = P(AXES)
    return jax.shard_map(
        body,
        mesh=Mesh(mesh.devices.reshape(SIZES), AXES),
        in_specs=(P(AXES, None), P(AXES, None), P(), every, P(), P()),
        out_specs=P(ROW, COL),
        check_vma=False,
    )
```

```python
import math

import jax
import jax.numpy as jnp
import ml_dtypes
import numpy as np
from jax import lax
from jax.experimental import pallas as pl
from jax.experimental.pallas import tpu as pltpu
from jax.sharding import Mesh, PartitionSpec as P

GRID = 72
STEPS = 2
AXES = ("z", "yl", "x", "yh", "c")
SIZES = (16, 2, 4, 2, 2)
ROW = ("z", "yl")
COL = ("x", "yh", "c")
PLANE = ("yl", "x", "yh", "c")
TILE = ("yl", "x", "yh")
QUAD = ("x", "yh")
LANES = 128
PIECE = 6
CHUNK = 16 * PIECE
SWAP = [(0, 1), (1, 0)]
REACH=12
KEPT=2*REACH+1
HALF=GRID//2
PAIR=GRID*GRID*2//LANES
ROWS=GRID**3//LANES
WIDE=16
BACK=32
SLOT=64
PAD_ROWS=40*PAIR


def exchange(x, axis):
    return lax.all_to_all(x, axis, split_axis=0, concat_axis=0, tiled=True)


def rows_kernel(flat, out, rows):
    done = ROWS // 32 * 32
    for at in range(0, done, 32):
        part = flat[:, at * LANES : (at + 32) * LANES].astype(jnp.float32)
        rows[at : at + 32, :] = part.reshape(32, LANES)
    part = flat[:, done * LANES :].astype(jnp.float32)
    rows[done:ROWS, :] = part.reshape(ROWS - done, LANES)
    rows[ROWS:, :] = jnp.zeros((32 * CHUNK - ROWS, LANES), jnp.float32)
    out[...] = rows[...].astype(jnp.bfloat16)


def in_rows(flat):
    return pl.pallas_call(
        rows_kernel,
        out_shape=jax.ShapeDtypeStruct((32 * CHUNK, LANES), jnp.bfloat16),
        in_specs=[pl.BlockSpec(memory_space=pltpu.VMEM)],
        out_specs=pl.BlockSpec(memory_space=pltpu.VMEM),
        scratch_shapes=[pltpu.VMEM((32 * CHUNK, LANES), jnp.float32)],
        cost_estimate=pl.CostEstimate(flops=0, bytes_accessed=4 * 2**20, transcendentals=0),
        compiler_params=pltpu.CompilerParams(vmem_limit_bytes=32 * 2**20),
    )(flat)


def from_owners(shard, owner):
    steps = owner.shape[0]
    owner_z, owner_plane = owner // 32, owner % 32
    parts = exchange(in_rows(shard).reshape(32, CHUNK, LANES), PLANE)
    parts = jnp.stack([lax.dynamic_index_in_dim(parts, owner_plane[s], 0, False) for s in range(steps)])
    parts = parts.reshape(steps, 16, PIECE, LANES).transpose(1, 0, 2, 3)
    parts = exchange(parts, "z")
    parts = jnp.stack([lax.dynamic_index_in_dim(parts[:, s], owner_z[s], 0, False) for s in range(steps)])
    parts = exchange(jnp.broadcast_to(parts[None], (16,) + parts.shape), "z")
    parts = parts.transpose(1, 0, 2, 3).reshape(steps * CHUNK, LANES)
    parts = exchange(jnp.broadcast_to(parts[None], (16,) + parts.shape), TILE)
    other = lax.ppermute(parts, "c", SWAP)
    first = lax.axis_index("c") == 0
    both = jnp.stack([jnp.where(first, parts, other), jnp.where(first, other, parts)], axis=1)
    both = both.reshape(32, steps, CHUNK, LANES).transpose(1, 0, 2, 3)
    return both.reshape(steps, 32 * CHUNK, LANES)


def split(x):
    high=x.astype(jnp.bfloat16)
    return high,(x-high.astype(jnp.float32)).astype(jnp.bfloat16)

def split_np(x):
    h=x.astype(ml_dtypes.bfloat16)
    return h,(x-h.astype(np.float64)).astype(ml_dtypes.bfloat16)

def tables():
    point=np.arange(GRID)
    def cs(freq):
        ang=2*math.pi*((freq[:,None]*point[None,:])%GRID)/GRID
        return np.cos(ang),np.sin(ang)
    c,s=cs(np.arange(REACH+1))
    t=np.zeros((2,WIDE,2,40))
    t[0,:REACH+1,0,:HALF]=c[:,0::2]; t[0,:REACH+1,1,:HALF]=c[:,1::2]
    t[1,:REACH+1,0,:HALF]=-s[:,0::2]; t[1,:REACH+1,1,:HALF]=-s[:,1::2]
    t=t.reshape(2*WIDE,80)
    h,l=split_np(t)
    first=np.concatenate([h,h,l],1)
    c,s=cs(np.arange(-REACH,REACH+1))
    w=np.zeros((2,LANES,2,SLOT))
    w[0,:GRID,0,:KEPT]=c.T; w[0,:GRID,1,:KEPT]=-s.T
    w[1,:GRID,0,:KEPT]=s.T; w[1,:GRID,1,:KEPT]=c.T
    w=w.reshape(2*LANES,LANES)
    h,l=split_np(w)
    third=np.concatenate([h,l],1)
    u=np.zeros((2,BACK,GRID))
    u[0,:KEPT]=c; u[1,:KEPT]=s
    u=u.reshape(2*BACK,GRID)
    h,l=split_np(u)
    second=np.concatenate([h,h,l],1)
    return first,second,third

def dft_kernel(scale, psi, cond, first, second, third, place, lane, sign, out, vals, held, mixed, spread):
    f32=jnp.float32; bf=jnp.bfloat16
    tail=PAD_ROWS-ROWS
    for s in range(STEPS):
        vals[s,:ROWS,:]=psi[s,:ROWS,:].astype(f32)*cond[:ROWS,:].astype(f32)
        vals[s,ROWS:,:]=jnp.zeros((tail,LANES),f32)
    left=lax.broadcasted_iota(jnp.int32,(40,LANES),1)<LANES//2
    table=first[...]
    zero=jnp.zeros((40,LANES),f32)
    rolled=[pltpu.roll(vals[s,pl.ds(40,40,stride=PAIR),:],LANES//2,1) for s in range(STEPS)]
    for t in range(41):
        cols=[]
        for s in range(STEPS):
            even=vals[s,pl.ds(t,40,stride=PAIR),:]
            here=rolled[s]
            ahead=pltpu.roll(vals[s,pl.ds(41+t,40,stride=PAIR),:],LANES//2,1) if t<40 else zero
            rolled[s]=ahead
            odd=jnp.where(left,here,ahead)
            x=jnp.concatenate([even,odd],0)
            h=x.astype(bf).astype(f32)
            cols.append(jnp.concatenate([h,x-h,h],0).astype(bf))
        y=jnp.dot(table,jnp.concatenate(cols,1),preferred_element_type=f32)
        for s in range(STEPS):
            held[s,:,t*LANES:(t+1)*LANES]=y[:,s*LANES:(s+1)*LANES]
    w=third[...]
    group=8
    for j0 in range(0,GRID,group):
        parts=[[],[]]
        for j in range(j0,j0+group):
            for s in range(STEPS):
                x=held[s,:,j*GRID:j*GRID+LANES]
                parts[0].append(x[:WIDE]); parts[1].append(x[WIDE:])
        x=jnp.concatenate([jnp.concatenate(parts[0],0),jnp.concatenate(parts[1],0)],1)
        h,l=split(x)
        y=jnp.dot(h,w,preferred_element_type=f32)
        z=jnp.dot(l,w[:,:LANES],preferred_element_type=f32)
        mixed[j0*32:(j0+group)*32,:]=y[:,:LANES]+y[:,LANES:]+z
    table=second[...]
    flip=jnp.where(lax.broadcasted_iota(jnp.int32,(BACK,LANES),1)<SLOT,1.0,-1.0).astype(f32)
    for i in range(REACH+1):
        cols=[]
        for s in range(STEPS):
            x=mixed[pl.ds(s*WIDE+i,GRID,stride=32),:]
            h=x.astype(bf).astype(f32)
            cols.append(jnp.concatenate([h,x-h,h],0).astype(bf))
        y=jnp.dot(table,jnp.concatenate(cols,1),preferred_element_type=f32)
        for s in range(STEPS):
            z=y[:,s*LANES:(s+1)*LANES]
            r=(z[:BACK]+flip*pltpu.roll(z[BACK:],SLOT,1))*scale[s]
            spread[s*LANES:(s+1)*LANES, i*BACK:(i+1)*BACK]=r.T.astype(bf)
    tile=512
    rows=(REACH+1)*BACK
    data=spread[...]
    at=lax.broadcasted_iota(jnp.int32,(rows,tile),0)
    slot=lax.broadcasted_iota(jnp.int32,(SLOT,tile),0)
    def pick(n,_):
        here=pl.ds(pl.multiple_of(n*tile,tile),tile)
        hot=jnp.where(at==place[:,here],1.0,0.0).astype(bf)
        y=jnp.dot(data,hot,preferred_element_type=f32)
        keep=slot==lane[:,here]
        r=[jnp.sum(jnp.where(keep,y[p*SLOT:(p+1)*SLOT],0.0),0,keepdims=True) for p in range(2*STEPS)]
        sg=sign[:,here]
        out[:,here]=jnp.concatenate([r[0],r[1]*sg,r[2],r[3]*sg],0).astype(bf)
        return 0
    lax.fori_loop(0,place.shape[1]//tile,pick,0)

def pairs(psi, cond, scale, g_index):
    third=g_index%GRID; second=g_index//GRID%GRID; first=g_index//(GRID*GRID)
    mid=GRID//2
    i=jnp.where(first<mid,first,first-GRID); j=jnp.where(second<mid,second,second-GRID); k=jnp.where(third<mid,third,third-GRID)
    sg=jnp.where(i<0,-1,1)
    place=i*sg*BACK+(j*sg+REACH)
    lane=k*sg+REACH
    a,b,c=[jnp.asarray(x) for x in tables()]
    ng=g_index.shape[0]
    vm=pl.BlockSpec(memory_space=pltpu.VMEM)
    return pl.pallas_call(dft_kernel,
        out_shape=jax.ShapeDtypeStruct((2*STEPS,ng),jnp.bfloat16),
        in_specs=[pl.BlockSpec(memory_space=pltpu.SMEM)]+[vm]*8,
        out_specs=vm,
        scratch_shapes=[pltpu.VMEM((STEPS,PAD_ROWS,LANES),jnp.float32),
            pltpu.VMEM((STEPS,2*WIDE,41*LANES),jnp.float32),
            pltpu.VMEM((GRID*32,LANES),jnp.float32),
            pltpu.VMEM((STEPS*LANES,(REACH+1)*BACK),jnp.bfloat16)],
        compiler_params=pltpu.CompilerParams(vmem_limit_bytes=48*2**20),
    )(scale,psi,cond,a,b,c,place[None],lane[None],sg.astype(jnp.float32)[None])


def body(valence, conduction, val_energy, cond_energy, owner, g_index):
    bands = STEPS * 512
    psi = from_owners(valence, owner)
    cond = in_rows(conduction)
    scale = jnp.sqrt(4.0 / (cond_energy[0] - val_energy[owner])) / math.sqrt(GRID**3)
    elems = pairs(psi, cond, scale, g_index)
    count = elems.shape[0]
    ng = elems.shape[1]
    rows = exchange(elems.reshape(count, 16, ng // 16).transpose(1, 0, 2), "z").transpose(1, 0, 2)
    rows = exchange(jnp.broadcast_to(rows[None], (8,) + rows.shape), QUAD)
    other = lax.ppermute(rows, "c", SWAP)
    first = lax.axis_index("c") == 0
    rows = jnp.stack([jnp.where(first, rows, other), jnp.where(first, other, rows)], axis=1)
    cols = exchange(elems.reshape(count, 16, ng // 16).transpose(1, 0, 2), COL).transpose(1, 0, 2)
    cols = exchange(jnp.broadcast_to(cols[None], (16,) + cols.shape), "z")
    cols = cols.reshape(16, count, 8, 2, ng // 16)
    part = jnp.einsum("mclzg,zlmch->gh", rows, cols, preferred_element_type=jnp.float32)
    part = part.reshape(2, ng // 32, ng // 16)
    mine = lax.axis_index("yl")
    away = lax.dynamic_index_in_dim(part, 1 - mine, 0, False).astype(jnp.bfloat16)
    here = lax.dynamic_index_in_dim(part, mine, 0, False)
    total = here + lax.ppermute(away, "yl", SWAP).astype(jnp.float32)
    return -total / math.sqrt(bands)


def solution(mesh):
    every = P(AXES)
    return jax.shard_map(
        body,
        mesh=Mesh(mesh.devices.reshape(SIZES), AXES),
        in_specs=(P(AXES, None), P(AXES, None), P(), every, P(), P()),
        out_specs=P(ROW, COL),
        check_vma=False,
    )
```

```python
import math

import jax
import jax.numpy as jnp
import ml_dtypes
import numpy as np
from jax import lax
from jax.experimental import pallas as pl
from jax.experimental.pallas import tpu as pltpu
from jax.sharding import Mesh, PartitionSpec as P

GRID = 72
STEPS = 2
AXES = ("z", "yl", "x", "yh", "c")
SIZES = (16, 2, 4, 2, 2)
ROW = ("z", "yl")
COL = ("x", "yh", "c")
PLANE = ("yl", "x", "yh", "c")
TILE = ("yl", "x", "yh")
QUAD = ("x", "yh")
LANES = 128
PIECE = 6
CHUNK = 16 * PIECE
SWAP = [(0, 1), (1, 0)]
NG = 8192
BLOCKS = 16
SPAN = NG // BLOCKS
SLOTS = 320
WIDTH = 384
BOTH = 2 * SLOTS // LANES
ELEMS = 16
NAMED = 1 << 20
REACH=12
KEPT=2*REACH+1
HALF=GRID//2
PAIR=GRID*GRID*2//LANES
ROWS=GRID**3//LANES
WIDE=16
BACK=32
SLOT=64
PAD_ROWS=40*PAIR


def exchange(x, axis):
    return lax.all_to_all(x, axis, split_axis=0, concat_axis=0, tiled=True)


def rows_kernel(flat, out, rows):
    done = ROWS // 32 * 32
    for at in range(0, done, 32):
        part = flat[:, at * LANES : (at + 32) * LANES].astype(jnp.float32)
        rows[at : at + 32, :] = part.reshape(32, LANES)
    part = flat[:, done * LANES :].astype(jnp.float32)
    rows[done:ROWS, :] = part.reshape(ROWS - done, LANES)
    rows[ROWS:, :] = jnp.zeros((32 * CHUNK - ROWS, LANES), jnp.float32)
    out[...] = rows[...].astype(jnp.bfloat16)


def in_rows(flat):
    return pl.pallas_call(
        rows_kernel,
        out_shape=jax.ShapeDtypeStruct((32 * CHUNK, LANES), jnp.bfloat16),
        in_specs=[pl.BlockSpec(memory_space=pltpu.VMEM)],
        out_specs=pl.BlockSpec(memory_space=pltpu.VMEM),
        scratch_shapes=[pltpu.VMEM((32 * CHUNK, LANES), jnp.float32)],
        cost_estimate=pl.CostEstimate(flops=0, bytes_accessed=4 * 2**20, transcendentals=0),
        compiler_params=pltpu.CompilerParams(vmem_limit_bytes=32 * 2**20),
    )(flat)


def from_owners(shard, owner):
    steps = owner.shape[0]
    owner_z, owner_plane = owner // 32, owner % 32
    parts = exchange(in_rows(shard).reshape(32, CHUNK, LANES), PLANE)
    parts = jnp.stack([lax.dynamic_index_in_dim(parts, owner_plane[s], 0, False) for s in range(steps)])
    parts = parts.reshape(steps, 16, PIECE, LANES).transpose(1, 0, 2, 3)
    parts = exchange(parts, "z")
    parts = jnp.stack([lax.dynamic_index_in_dim(parts[:, s], owner_z[s], 0, False) for s in range(steps)])
    parts = exchange(jnp.broadcast_to(parts[None], (16,) + parts.shape), "z")
    parts = parts.transpose(1, 0, 2, 3).reshape(steps * CHUNK, LANES)
    parts = exchange(jnp.broadcast_to(parts[None], (16,) + parts.shape), TILE)
    other = lax.ppermute(parts, "c", SWAP)
    first = lax.axis_index("c") == 0
    both = jnp.stack([jnp.where(first, parts, other), jnp.where(first, other, parts)], axis=1)
    both = both.reshape(32, steps, CHUNK, LANES).transpose(1, 0, 2, 3)
    return both.reshape(steps, 32 * CHUNK, LANES)


def split(x):
    high=x.astype(jnp.bfloat16)
    return high,(x-high.astype(jnp.float32)).astype(jnp.bfloat16)

def split_np(x):
    h=x.astype(ml_dtypes.bfloat16)
    return h,(x-h.astype(np.float64)).astype(ml_dtypes.bfloat16)

def tables():
    point=np.arange(GRID)
    def cs(freq):
        ang=2*math.pi*((freq[:,None]*point[None,:])%GRID)/GRID
        return np.cos(ang),np.sin(ang)
    c,s=cs(np.arange(REACH+1))
    t=np.zeros((2,WIDE,2,40))
    t[0,:REACH+1,0,:HALF]=c[:,0::2]; t[0,:REACH+1,1,:HALF]=c[:,1::2]
    t[1,:REACH+1,0,:HALF]=-s[:,0::2]; t[1,:REACH+1,1,:HALF]=-s[:,1::2]
    t=t.reshape(2*WIDE,80)
    h,l=split_np(t)
    first=np.concatenate([h,h,l],1)
    c,s=cs(np.arange(-REACH,REACH+1))
    w=np.zeros((2,LANES,2,SLOT))
    w[0,:GRID,0,:KEPT]=c.T; w[0,:GRID,1,:KEPT]=-s.T
    w[1,:GRID,0,:KEPT]=s.T; w[1,:GRID,1,:KEPT]=c.T
    w=w.reshape(2*LANES,LANES)
    h,l=split_np(w)
    third=np.concatenate([h,l],1)
    u=np.zeros((2,BACK,GRID))
    u[0,:KEPT]=c; u[1,:KEPT]=s
    u=u.reshape(2*BACK,GRID)
    h,l=split_np(u)
    second=np.concatenate([h,h,l],1)
    return first,second,third

def dft_kernel(scale, psi, cond, first, second, third, places, out, vals, held, mixed, spread):
    f32=jnp.float32; bf=jnp.bfloat16
    tail=PAD_ROWS-ROWS
    for s in range(STEPS):
        vals[s,:ROWS,:]=psi[s,:ROWS,:].astype(f32)*cond[:ROWS,:].astype(f32)
        vals[s,ROWS:,:]=jnp.zeros((tail,LANES),f32)
    left=lax.broadcasted_iota(jnp.int32,(40,LANES),1)<LANES//2
    table=first[...]
    zero=jnp.zeros((40,LANES),f32)
    rolled=[pltpu.roll(vals[s,pl.ds(40,40,stride=PAIR),:],LANES//2,1) for s in range(STEPS)]
    for t in range(41):
        cols=[]
        for s in range(STEPS):
            even=vals[s,pl.ds(t,40,stride=PAIR),:]
            here=rolled[s]
            ahead=pltpu.roll(vals[s,pl.ds(41+t,40,stride=PAIR),:],LANES//2,1) if t<40 else zero
            rolled[s]=ahead
            odd=jnp.where(left,here,ahead)
            x=jnp.concatenate([even,odd],0)
            h=x.astype(bf).astype(f32)
            cols.append(jnp.concatenate([h,x-h,h],0).astype(bf))
        y=jnp.dot(table,jnp.concatenate(cols,1),preferred_element_type=f32)
        for s in range(STEPS):
            held[s,:,t*LANES:(t+1)*LANES]=y[:,s*LANES:(s+1)*LANES]
    w=third[...]
    group=8
    for j0 in range(0,GRID,group):
        parts=[[],[]]
        for j in range(j0,j0+group):
            for s in range(STEPS):
                x=held[s,:,j*GRID:j*GRID+LANES]
                parts[0].append(x[:WIDE]); parts[1].append(x[WIDE:])
        x=jnp.concatenate([jnp.concatenate(parts[0],0),jnp.concatenate(parts[1],0)],1)
        h,l=split(x)
        y=jnp.dot(h,w,preferred_element_type=f32)
        z=jnp.dot(l,w[:,:LANES],preferred_element_type=f32)
        mixed[j0*32:(j0+group)*32,:]=y[:,:LANES]+y[:,LANES:]+z
    table=second[...]
    flip=jnp.where(lax.broadcasted_iota(jnp.int32,(BACK,LANES),1)<SLOT,1.0,-1.0).astype(f32)
    for i in range(REACH+1):
        cols=[]
        for s in range(STEPS):
            x=mixed[pl.ds(s*WIDE+i,GRID,stride=32),:]
            h=x.astype(bf).astype(f32)
            cols.append(jnp.concatenate([h,x-h,h],0).astype(bf))
        y=jnp.dot(table,jnp.concatenate(cols,1),preferred_element_type=f32)
        for s in range(STEPS):
            z=y[:,s*LANES:(s+1)*LANES]
            r=(z[:BACK]+flip*pltpu.roll(z[BACK:],SLOT,1))*scale[s]
            spread[s*LANES:(s+1)*LANES, i*BACK:(i+1)*BACK]=r.T.astype(bf)
    rows = (REACH + 1) * BACK
    data = spread[...]
    at = lax.broadcasted_iota(jnp.int32, (rows, WIDTH), 0)
    slot = lax.broadcasted_iota(jnp.int32, (SLOT, WIDTH), 0)
    gap = jnp.zeros((STEPS, 2 * LANES), f32)
    for b in range(BLOCKS):
        place = places[b : b + 1, :]
        hot = jnp.where(at == (place >> 6), 1.0, 0.0).astype(bf)
        y = jnp.dot(data, hot, preferred_element_type=f32)
        keep = slot == (place & (SLOT - 1))
        got = [
            jnp.sum(jnp.where(keep, y[p * SLOT : (p + 1) * SLOT], 0.0), 0, keepdims=True)
            for p in range(2 * STEPS)
        ]
        real = jnp.concatenate([jnp.concatenate(got[0::2], 0), gap], 1)
        imag = pltpu.roll(jnp.concatenate(got[1::2], 0), WIDTH - SLOTS, 1)
        both = real + jnp.concatenate([gap, imag], 1)
        lines = [both[s : s + 1, n * LANES : (n + 1) * LANES] for s in range(STEPS) for n in range(BOTH)]
        lines.append(jnp.zeros((ELEMS - len(lines), LANES), f32))
        out[b] = jnp.concatenate(lines, 0).astype(bf)


def layout():
    axis = np.arange(-REACH, REACH + 1)
    grid = np.stack(np.meshgrid(axis, axis, axis, indexing="ij"), -1).reshape(-1, 3)
    length = (grid**2).sum(1)
    fixed = np.full((BLOCKS, WIDTH), -1)
    kind = np.zeros((BLOCKS, WIDTH), np.int32)
    target = np.full((BLOCKS, SPAN), -1)
    own = np.full((BLOCKS, WIDTH), -5)
    begin = [0] * BLOCKS
    shells = [[] for _ in range(BLOCKS)]
    ends = [0] * BLOCKS
    at = 0
    for value in np.unique(length):
        if at >= NG:
            break
        shell = grid[length == value]
        stop = min(at + len(shell), NG)
        for b in range(at // SPAN, (stop - 1) // SPAN + 1):
            low, high = max(at, b * SPAN), min(stop, b * SPAN + SPAN)
            if high - low == len(shell) or 2 * (high - low) > len(shell):
                i, j, k = shell.T
                front = (i > 0) | ((i == 0) & ((j > 0) | ((j == 0) & (k >= 0))))
                i, j, k = shell[front].T
                shells[b].append((i * BACK + j + REACH) * SLOT + k + REACH)
            elif low == b * SPAN:
                begin[b] = high - low
            else:
                assert high == b * SPAN + SPAN
                ends[b] = high - low
        at = stop
    for b in range(BLOCKS):
        known = np.concatenate(shells[b])
        assert begin[b] + len(known) + ends[b] <= SLOTS
        fixed[b, begin[b] : begin[b] + len(known)] = known
        own[b, begin[b] : begin[b] + len(known)] = known
        kind[b, : begin[b]] = 1
        kind[b, SLOTS - ends[b] : SLOTS] = 2
        target[b, : begin[b]] = NAMED + np.arange(begin[b])
        target[b, SPAN - ends[b] :] = NAMED + np.arange(SLOTS - ends[b], SLOTS)
        places = np.arange(WIDTH)
        own[b] = np.where(kind[b] > 0, NAMED + places, own[b])
    columns = np.full((2, WIDTH, LANES), -5.0, np.float32)
    columns[0, :, :BLOCKS] = own.T
    columns[1, SLOT:, :BLOCKS] = own.T[: WIDTH - SLOT]
    return fixed.astype(np.int32), kind, target.astype(np.int32), columns


def frequencies(g_index):
    fixed, kind, target, _ = layout()
    g = g_index.reshape(BLOCKS, SPAN)
    half = GRID // 2
    i, j, k = g // (GRID * GRID), g // GRID % GRID, g % GRID
    i, j, k = [jnp.where(n < half, n, n - GRID) for n in (i, j, k)]
    front = (i > 0) | ((i == 0) & ((j > 0) | ((j == 0) & (k >= 0))))
    sign = jnp.where(front, 1, -1)
    ids = (i * sign * BACK + j * sign + REACH) * SLOT + k * sign + REACH
    first = ids[:, :WIDTH]
    last = jnp.pad(ids[:, SPAN - SLOTS :], ((0, 0), (0, WIDTH - SLOTS)))
    places = jnp.where(kind == 1, first, jnp.where(kind == 2, last, fixed))
    names = jnp.where(target >= 0, target, ids)
    return places, names.astype(jnp.float32), sign.astype(jnp.float32)


def pairs(psi, cond, scale, places):
    first, second, third = [jnp.asarray(table) for table in (tables())]
    vm = pl.BlockSpec(memory_space=pltpu.VMEM)
    return pl.pallas_call(
        dft_kernel,
        out_shape=jax.ShapeDtypeStruct((BLOCKS, ELEMS, LANES), jnp.bfloat16),
        in_specs=[pl.BlockSpec(memory_space=pltpu.SMEM)] + [vm] * 6,
        out_specs=vm,
        scratch_shapes=[
            pltpu.VMEM((STEPS, PAD_ROWS, LANES), jnp.float32),
            pltpu.VMEM((STEPS, 2 * WIDE, 41 * LANES), jnp.float32),
            pltpu.VMEM((GRID * 32, LANES), jnp.float32),
            pltpu.VMEM((STEPS * LANES, (REACH + 1) * BACK), jnp.bfloat16),
        ],
        compiler_params=pltpu.CompilerParams(vmem_limit_bytes=48 * 2**20),
    )(scale, psi, cond, first, second, third, places)


def sums_kernel(me, same, other, cols, names, signs, columns, here, away):
    f32, bf = jnp.float32, jnp.bfloat16
    z, m, yl, c = [me[n] for n in range(4)]
    half = SPAN // 2

    def spread(block, swapped):
        name, sign = names[pl.ds(block, 1), :], signs[pl.ds(block, 1), :]
        if swapped is not None:
            turn = lambda x: jnp.where(swapped, jnp.concatenate([x[:, half:], x[:, :half]], 1), x)
            name, sign = turn(name), turn(sign)
        chosen = lax.broadcasted_iota(jnp.int32, (WIDTH, LANES), 1) == block
        place = [jnp.sum(jnp.where(chosen, columns[p], 0.0), 1, keepdims=True) for p in range(2)]
        real = jnp.where(place[0] == name, 1.0, 0.0).astype(bf)
        return real, jnp.where(place[1] == name, sign, 0.0).astype(bf)

    def lanes(ref, n):
        return ref[:, n * 32 : (n + 1) * 32, :].reshape(-1, LANES)

    def widened(tiles, hot):
        real = jnp.dot(jnp.concatenate(tiles[:3], 1), hot[0], preferred_element_type=f32)
        imag = jnp.dot(jnp.concatenate(tiles[2:], 1), hot[1], preferred_element_type=f32)
        return real.astype(bf), imag.astype(bf)

    count = cols.shape[0] * 32
    to = lax.broadcasted_iota(jnp.int32, (count, count), 0)
    at = lax.broadcasted_iota(jnp.int32, (count, count), 1)
    core = jnp.bitwise_xor(at >> 8, c)
    order = ((at & 15) << 5) | (((at >> 4) & 1) << 4) | (((at >> 5) & 7) << 1) | core
    order = jnp.where(to == order, 1.0, 0.0).astype(bf)
    tiles = [jnp.concatenate([lanes(same, n), lanes(other, n)], 0) for n in range(BOTH)]
    tiles = jnp.dot(order, jnp.concatenate(tiles, 1), preferred_element_type=f32).astype(bf)
    tiles = [tiles[:, n * LANES : (n + 1) * LANES] for n in range(BOTH)]
    left = widened(tiles, spread(z, yl == 1))
    right = widened([lanes(cols, n) for n in range(BOTH)], spread(m, None))
    over = (((0,), (0,)), ((), ()))
    total = lax.dot_general(left[0], right[0], over, preferred_element_type=f32)
    total += lax.dot_general(left[1], right[1], over, preferred_element_type=f32)
    total *= -1.0 / math.sqrt(STEPS * 512)
    here[...] = total[:half]
    away[...] = total[half:].astype(bf)


def sums(me, same, other, cols, names, signs):
    vm = pl.BlockSpec(memory_space=pltpu.VMEM)
    half = SPAN // 2
    return pl.pallas_call(
        sums_kernel,
        out_shape=[
            jax.ShapeDtypeStruct((half, SPAN), jnp.float32),
            jax.ShapeDtypeStruct((half, SPAN), jnp.bfloat16),
        ],
        in_specs=[pl.BlockSpec(memory_space=pltpu.SMEM)] + [vm] * 6,
        out_specs=[vm, vm],
        compiler_params=pltpu.CompilerParams(vmem_limit_bytes=48 * 2**20),
    )(me, same, other, cols, names, signs, jnp.asarray(layout()[3]))


def body(valence, conduction, val_energy, cond_energy, owner, g_index):
    psi = from_owners(valence, owner)
    cond = in_rows(conduction)
    scale = jnp.sqrt(4.0 / (cond_energy[0] - val_energy[owner])) / math.sqrt(GRID**3)
    places, names, signs = frequencies(g_index)
    elems = pairs(psi, cond, scale, places)

    def by_lanes(x):
        return x.reshape(16, STEPS, BOTH, LANES).transpose(2, 1, 0, 3).reshape(16 * STEPS * BOTH, LANES)

    used = STEPS * BOTH
    cols = by_lanes(exchange(elems, COL)[:, :used])
    cols = jnp.broadcast_to(cols[None], (16,) + cols.shape)
    cols = exchange(jnp.concatenate([cols, elems], axis=1), "z")
    rows = by_lanes(cols[:, -ELEMS : used - ELEMS])
    rows = exchange(jnp.broadcast_to(rows[None], (8,) + rows.shape), QUAD)
    other = lax.ppermute(rows, "c", SWAP)
    me = jnp.stack([lax.axis_index(a) for a in ("z", COL, "yl", "c")]).astype(jnp.int32)
    here, away = sums(me, rows, other, cols, names, signs)
    return here + lax.ppermute(away, "yl", SWAP).astype(jnp.float32)


def solution(mesh):
    every = P(AXES)
    return jax.shard_map(
        body,
        mesh=Mesh(mesh.devices.reshape(SIZES), AXES),
        in_specs=(P(AXES, None), P(AXES, None), P(), every, P(), P()),
        out_specs=P(ROW, COL),
        check_vma=False,
    )
```

```python
import math

import jax
import jax.numpy as jnp
import ml_dtypes
import numpy as np
from jax import lax
from jax.experimental import pallas as pl
from jax.experimental.pallas import tpu as pltpu
from jax.sharding import Mesh, PartitionSpec as P

GRID = 72
STEPS = 2
AXES = ("z", "yl", "x", "yh", "c")
SIZES = (16, 2, 4, 2, 2)
ROW = ("z", "yl")
COL = ("x", "yh", "c")
PLANE = ("yl", "x", "yh", "c")
TILE = ("yl", "x", "yh")
QUAD = ("x", "yh")
LANES = 128
PIECE = 6
CHUNK = 16 * PIECE
SWAP = [(0, 1), (1, 0)]
NG = 8192
BLOCKS = 16
SPAN = NG // BLOCKS
SLOTS = 320
WIDTH = 384
BOTH = 2 * SLOTS // LANES
LINES = STEPS * BOTH
ELEMS = LINES * BLOCKS
NAMED = 1 << 20
REACH=12
KEPT=2*REACH+1
HALF=GRID//2
PAIR=GRID*GRID*2//LANES
ROWS=GRID**3//LANES
WIDE=16
BACK=32
SLOT=64
PAD_ROWS=40*PAIR


def exchange(x, axis):
    return lax.all_to_all(x, axis, split_axis=0, concat_axis=0, tiled=True)


def rows_kernel(flat, out, rows):
    done = ROWS // 32 * 32
    for at in range(0, done, 32):
        part = flat[:, at * LANES : (at + 32) * LANES].astype(jnp.float32)
        rows[at : at + 32, :] = part.reshape(32, LANES)
    part = flat[:, done * LANES :].astype(jnp.float32)
    rows[done:ROWS, :] = part.reshape(ROWS - done, LANES)
    rows[ROWS:, :] = jnp.zeros((32 * CHUNK - ROWS, LANES), jnp.float32)
    out[...] = rows[...].astype(jnp.bfloat16)


def in_rows(flat):
    return pl.pallas_call(
        rows_kernel,
        out_shape=jax.ShapeDtypeStruct((32 * CHUNK, LANES), jnp.bfloat16),
        in_specs=[pl.BlockSpec(memory_space=pltpu.VMEM)],
        out_specs=pl.BlockSpec(memory_space=pltpu.VMEM),
        scratch_shapes=[pltpu.VMEM((32 * CHUNK, LANES), jnp.float32)],
        cost_estimate=pl.CostEstimate(flops=0, bytes_accessed=4 * 2**20, transcendentals=0),
        compiler_params=pltpu.CompilerParams(vmem_limit_bytes=32 * 2**20),
    )(flat)


def from_owners(shard, owner):
    steps = owner.shape[0]
    owner_z, owner_plane = owner // 32, owner % 32
    parts = exchange(in_rows(shard).reshape(32, CHUNK, LANES), PLANE)
    parts = jnp.stack([lax.dynamic_index_in_dim(parts, owner_plane[s], 0, False) for s in range(steps)])
    parts = parts.reshape(steps, 16, PIECE, LANES).transpose(1, 0, 2, 3)
    parts = exchange(parts, "z")
    parts = jnp.stack([lax.dynamic_index_in_dim(parts[:, s], owner_z[s], 0, False) for s in range(steps)])
    parts = exchange(jnp.broadcast_to(parts[None], (16,) + parts.shape), "z")
    parts = parts.transpose(1, 0, 2, 3).reshape(steps * CHUNK, LANES)
    parts = exchange(jnp.broadcast_to(parts[None], (16,) + parts.shape), TILE)
    return parts, lax.ppermute(parts, "c", SWAP)


def split(x):
    high=x.astype(jnp.bfloat16)
    return high,(x-high.astype(jnp.float32)).astype(jnp.bfloat16)

def split_np(x):
    h=x.astype(ml_dtypes.bfloat16)
    return h,(x-h.astype(np.float64)).astype(ml_dtypes.bfloat16)

def tables():
    point=np.arange(GRID)
    def cs(freq):
        ang=2*math.pi*((freq[:,None]*point[None,:])%GRID)/GRID
        return np.cos(ang),np.sin(ang)
    c,s=cs(np.arange(REACH+1))
    t=np.zeros((2,WIDE,2,40))
    t[0,:REACH+1,0,:HALF]=c[:,0::2]; t[0,:REACH+1,1,:HALF]=c[:,1::2]
    t[1,:REACH+1,0,:HALF]=-s[:,0::2]; t[1,:REACH+1,1,:HALF]=-s[:,1::2]
    t=t.reshape(2*WIDE,80)
    h,l=split_np(t)
    first=np.concatenate([h,h,l],1)
    c,s=cs(np.arange(-REACH,REACH+1))
    w=np.zeros((2,LANES,2,SLOT))
    w[0,:GRID,0,:KEPT]=c.T; w[0,:GRID,1,:KEPT]=-s.T
    w[1,:GRID,0,:KEPT]=s.T; w[1,:GRID,1,:KEPT]=c.T
    w=w.reshape(2*LANES,LANES)
    h,l=split_np(w)
    third=np.concatenate([h,l],1)
    u=np.zeros((2,BACK,GRID))
    u[0,:KEPT]=c; u[1,:KEPT]=s
    u=u.reshape(2*BACK,GRID)
    h,l=split_np(u)
    second=np.concatenate([h,h,l],1)
    return first,second,third

def dft_kernel(core, scale, same, other, cond, first, second, third, places, out, vals, held, mixed, spread, lined):
    f32=jnp.float32; bf=jnp.bfloat16
    for s in range(STEPS):
        vals[s, 32 * CHUNK :, :] = jnp.zeros((PAD_ROWS - 32 * CHUNK, LANES), f32)
        for t in range(16):
            for psi, side in ((same, core[0]), (other, 1 - core[0])):
                here = pl.ds(pl.multiple_of((2 * t + side) * CHUNK, CHUNK), CHUNK)
                band = psi[t, s * CHUNK : (s + 1) * CHUNK, :].astype(f32)
                vals[s, here, :] = band * cond[here, :].astype(f32)
    left=lax.broadcasted_iota(jnp.int32,(40,LANES),1)<LANES//2
    table=first[...]
    zero=jnp.zeros((40,LANES),f32)
    rolled=[pltpu.roll(vals[s,pl.ds(40,40,stride=PAIR),:],LANES//2,1) for s in range(STEPS)]
    for t in range(41):
        cols=[]
        for s in range(STEPS):
            even=vals[s,pl.ds(t,40,stride=PAIR),:]
            here=rolled[s]
            ahead=pltpu.roll(vals[s,pl.ds(41+t,40,stride=PAIR),:],LANES//2,1) if t<40 else zero
            rolled[s]=ahead
            odd=jnp.where(left,here,ahead)
            x=jnp.concatenate([even,odd],0)
            h=x.astype(bf).astype(f32)
            cols.append(jnp.concatenate([h,x-h,h],0).astype(bf))
        y=jnp.dot(table,jnp.concatenate(cols,1),preferred_element_type=f32)
        for s in range(STEPS):
            held[s,:,t*LANES:(t+1)*LANES]=y[:,s*LANES:(s+1)*LANES]
    w=third[...]
    group=8
    for j0 in range(0,GRID,group):
        parts=[[],[]]
        for j in range(j0,j0+group):
            for s in range(STEPS):
                x=held[s,:,j*GRID:j*GRID+LANES]
                parts[0].append(x[:WIDE]); parts[1].append(x[WIDE:])
        x=jnp.concatenate([jnp.concatenate(parts[0],0),jnp.concatenate(parts[1],0)],1)
        h,l=split(x)
        y=jnp.dot(h,w,preferred_element_type=f32)
        z=jnp.dot(l,w[:,:LANES],preferred_element_type=f32)
        mixed[j0*32:(j0+group)*32,:]=y[:,:LANES]+y[:,LANES:]+z
    table=second[...]
    flip=jnp.where(lax.broadcasted_iota(jnp.int32,(BACK,LANES),1)<SLOT,1.0,-1.0).astype(f32)
    for i in range(REACH+1):
        cols=[]
        for s in range(STEPS):
            x=mixed[pl.ds(s*WIDE+i,GRID,stride=32),:]
            h=x.astype(bf).astype(f32)
            cols.append(jnp.concatenate([h,x-h,h],0).astype(bf))
        y=jnp.dot(table,jnp.concatenate(cols,1),preferred_element_type=f32)
        for s in range(STEPS):
            z=y[:,s*LANES:(s+1)*LANES]
            r=(z[:BACK]+flip*pltpu.roll(z[BACK:],SLOT,1))*scale[s]
            spread[s*LANES:(s+1)*LANES, i*BACK:(i+1)*BACK]=r.T.astype(bf)
    rows = (REACH + 1) * BACK
    data = spread[...]
    at = lax.broadcasted_iota(jnp.int32, (rows, WIDTH), 0)
    slot = lax.broadcasted_iota(jnp.int32, (SLOT, WIDTH), 0)
    gap = jnp.zeros((STEPS, 2 * LANES), f32)
    for b in range(BLOCKS):
        place = places[b : b + 1, :]
        hot = jnp.where(at == (place >> 6), 1.0, 0.0).astype(bf)
        y = jnp.dot(data, hot, preferred_element_type=f32)
        keep = slot == (place & (SLOT - 1))
        got = [
            jnp.sum(jnp.where(keep, y[p * SLOT : (p + 1) * SLOT], 0.0), 0, keepdims=True)
            for p in range(2 * STEPS)
        ]
        real = jnp.concatenate([jnp.concatenate(got[0::2], 0), gap], 1)
        imag = pltpu.roll(jnp.concatenate(got[1::2], 0), WIDTH - SLOTS, 1)
        both = real + jnp.concatenate([gap, imag], 1)
        for s in range(STEPS):
            for n in range(BOTH):
                at_line = (s * BOTH + n) * BLOCKS + b
                lined[at_line : at_line + 1, :] = both[s : s + 1, n * LANES : (n + 1) * LANES]
    out[...] = lined[...].astype(bf)


def turn_kernel(block, gathered, out, rows):
    rows[...] = gathered[...].astype(jnp.float32)
    for b in range(BLOCKS):
        for line in range(LINES):
            s, n = line // BOTH, line % BOTH
            got = rows[pl.ds(line * BLOCKS + b, 16, stride=ELEMS), :]
            to = (n * STEPS + s) * 16
            out[b, to : to + 16, :] = got.astype(jnp.bfloat16)
    chosen = out[block[0], :ELEMS, :]
    for b in range(BLOCKS):
        out[b, ELEMS:, :] = chosen


def turn(block, gathered):
    vm = pl.BlockSpec(memory_space=pltpu.VMEM)
    return pl.pallas_call(
        turn_kernel,
        out_shape=jax.ShapeDtypeStruct((BLOCKS, 2 * ELEMS, LANES), jnp.bfloat16),
        in_specs=[pl.BlockSpec(memory_space=pltpu.SMEM), vm],
        out_specs=vm,
        scratch_shapes=[pltpu.VMEM((16 * ELEMS, LANES), jnp.float32)],
        compiler_params=pltpu.CompilerParams(vmem_limit_bytes=32 * 2**20),
    )(block, gathered)


def layout():
    axis = np.arange(-REACH, REACH + 1)
    grid = np.stack(np.meshgrid(axis, axis, axis, indexing="ij"), -1).reshape(-1, 3)
    length = (grid**2).sum(1)
    fixed = np.full((BLOCKS, WIDTH), -1)
    kind = np.zeros((BLOCKS, WIDTH), np.int32)
    target = np.full((BLOCKS, SPAN), -1)
    own = np.full((BLOCKS, WIDTH), -5)
    begin = [0] * BLOCKS
    shells = [[] for _ in range(BLOCKS)]
    ends = [0] * BLOCKS
    at = 0
    for value in np.unique(length):
        if at >= NG:
            break
        shell = grid[length == value]
        stop = min(at + len(shell), NG)
        for b in range(at // SPAN, (stop - 1) // SPAN + 1):
            low, high = max(at, b * SPAN), min(stop, b * SPAN + SPAN)
            if high - low == len(shell) or 2 * (high - low) > len(shell):
                i, j, k = shell.T
                front = (i > 0) | ((i == 0) & ((j > 0) | ((j == 0) & (k >= 0))))
                i, j, k = shell[front].T
                shells[b].append((i * BACK + j + REACH) * SLOT + k + REACH)
            elif low == b * SPAN:
                begin[b] = high - low
            else:
                assert high == b * SPAN + SPAN
                ends[b] = high - low
        at = stop
    for b in range(BLOCKS):
        known = np.concatenate(shells[b])
        assert begin[b] + len(known) + ends[b] <= SLOTS
        fixed[b, begin[b] : begin[b] + len(known)] = known
        own[b, begin[b] : begin[b] + len(known)] = known
        kind[b, : begin[b]] = 1
        kind[b, SLOTS - ends[b] : SLOTS] = 2
        target[b, : begin[b]] = NAMED + np.arange(begin[b])
        target[b, SPAN - ends[b] :] = NAMED + np.arange(SLOTS - ends[b], SLOTS)
        places = np.arange(WIDTH)
        own[b] = np.where(kind[b] > 0, NAMED + places, own[b])
    columns = np.full((2, WIDTH, LANES), -5.0, np.float32)
    columns[0, :, :BLOCKS] = own.T
    columns[1, SLOT:, :BLOCKS] = own.T[: WIDTH - SLOT]
    return fixed.astype(np.int32), kind, target.astype(np.int32), columns


def frequencies(g_index):
    fixed, kind, target, _ = layout()
    g = g_index.reshape(BLOCKS, SPAN)
    half = GRID // 2
    i, j, k = g // (GRID * GRID), g // GRID % GRID, g % GRID
    i, j, k = [jnp.where(n < half, n, n - GRID) for n in (i, j, k)]
    front = (i > 0) | ((i == 0) & ((j > 0) | ((j == 0) & (k >= 0))))
    sign = jnp.where(front, 1, -1)
    ids = (i * sign * BACK + j * sign + REACH) * SLOT + k * sign + REACH
    first = ids[:, :WIDTH]
    last = jnp.pad(ids[:, SPAN - SLOTS :], ((0, 0), (0, WIDTH - SLOTS)))
    places = jnp.where(kind == 1, first, jnp.where(kind == 2, last, fixed))
    names = jnp.where(target >= 0, target, ids)
    return places, names.astype(jnp.float32), sign.astype(jnp.float32)


def pairs(psi, cond, scale, places, core):
    first, second, third = [jnp.asarray(table) for table in (tables())]
    vm = pl.BlockSpec(memory_space=pltpu.VMEM)
    return pl.pallas_call(
        dft_kernel,
        out_shape=jax.ShapeDtypeStruct((ELEMS, LANES), jnp.bfloat16),
        in_specs=[pl.BlockSpec(memory_space=pltpu.SMEM)] * 2 + [vm] * 7,
        out_specs=vm,
        scratch_shapes=[
            pltpu.VMEM((STEPS, PAD_ROWS, LANES), jnp.float32),
            pltpu.VMEM((STEPS, 2 * WIDE, 41 * LANES), jnp.float32),
            pltpu.VMEM((GRID * 32, LANES), jnp.float32),
            pltpu.VMEM((STEPS * LANES, (REACH + 1) * BACK), jnp.bfloat16),
            pltpu.VMEM((ELEMS, LANES), jnp.float32),
        ],
        compiler_params=pltpu.CompilerParams(vmem_limit_bytes=48 * 2**20),
    )(core, scale, *psi, cond, first, second, third, places)


def sums_kernel(me, elems, names, signs, columns, here, away):
    f32, bf = jnp.float32, jnp.bfloat16
    z, m, yl = [me[n] for n in range(3)]
    half = SPAN // 2

    def spread(block, swapped):
        name, sign = names[pl.ds(block, 1), :], signs[pl.ds(block, 1), :]
        if swapped is not None:
            turn = lambda x: jnp.where(swapped, jnp.concatenate([x[:, half:], x[:, :half]], 1), x)
            name, sign = turn(name), turn(sign)
        chosen = lax.broadcasted_iota(jnp.int32, (WIDTH, LANES), 1) == block
        place = [jnp.sum(jnp.where(chosen, columns[p], 0.0), 1, keepdims=True) for p in range(2)]
        real = jnp.where(place[0] == name, 1.0, 0.0).astype(bf)
        return real, jnp.where(place[1] == name, sign, 0.0).astype(bf)

    def lanes(n):
        return elems[:, n * 32 : (n + 1) * 32, :].reshape(-1, LANES)

    def widened(tiles, hot):
        real = jnp.dot(jnp.concatenate(tiles[:3], 1), hot[0], preferred_element_type=f32)
        imag = jnp.dot(jnp.concatenate(tiles[2:], 1), hot[1], preferred_element_type=f32)
        return real.astype(bf), imag.astype(bf)

    left = widened([lanes(BOTH + n) for n in range(BOTH)], spread(z, yl == 1))
    right = widened([lanes(n) for n in range(BOTH)], spread(m, None))
    over = (((0,), (0,)), ((), ()))
    total = lax.dot_general(left[0], right[0], over, preferred_element_type=f32)
    total += lax.dot_general(left[1], right[1], over, preferred_element_type=f32)
    total *= -1.0 / math.sqrt(STEPS * 512)
    here[...] = total[:half]
    away[...] = total[half:].astype(bf)


def sums(me, elems, names, signs):
    vm = pl.BlockSpec(memory_space=pltpu.VMEM)
    half = SPAN // 2
    return pl.pallas_call(
        sums_kernel,
        out_shape=[
            jax.ShapeDtypeStruct((half, SPAN), jnp.float32),
            jax.ShapeDtypeStruct((half, SPAN), jnp.bfloat16),
        ],
        in_specs=[pl.BlockSpec(memory_space=pltpu.SMEM)] + [vm] * 4,
        out_specs=[vm, vm],
        compiler_params=pltpu.CompilerParams(vmem_limit_bytes=48 * 2**20),
    )(me, elems, names, signs, jnp.asarray(layout()[3]))


def body(valence, conduction, val_energy, cond_energy, owner, g_index):
    psi = from_owners(valence, owner)
    cond = in_rows(conduction)
    scale = jnp.sqrt(4.0 / (cond_energy[0] - val_energy[owner])) / math.sqrt(GRID**3)
    places, names, signs = frequencies(g_index)
    core = lax.axis_index("c").astype(jnp.int32)
    elems = pairs(psi, cond, scale, places, core[None])

    elems = lax.all_gather(elems, "z", axis=0, tiled=True)
    me = jnp.stack([lax.axis_index(a) for a in ("z", COL, "yl")]).astype(jnp.int32)
    elems = exchange(turn(me, elems), COL)
    here, away = sums(me, elems, names, signs)
    return here + lax.ppermute(away, "yl", SWAP).astype(jnp.float32)


def solution(mesh):
    every = P(AXES)
    return jax.shard_map(
        body,
        mesh=Mesh(mesh.devices.reshape(SIZES), AXES),
        in_specs=(P(AXES, None), P(AXES, None), P(), every, P(), P()),
        out_specs=P(ROW, COL),
        check_vma=False,
    )
```

```python
import math

import jax
import jax.numpy as jnp
import ml_dtypes
import numpy as np
from jax import lax
from jax.experimental import pallas as pl
from jax.experimental.pallas import tpu as pltpu
from jax.sharding import Mesh, PartitionSpec as P

GRID = 72
STEPS = 2
AXES = ("z", "yl", "x", "yh", "c")
SIZES = (16, 2, 4, 2, 2)
ROW = ("z", "yl")
COL = ("x", "yh", "c")
PLANE = ("yl", "x", "yh", "c")
TILE = ("yl", "x", "yh")
QUAD = ("x", "yh")
LANES = 128
PIECE = 6
CHUNK = 16 * PIECE
SWAP = [(0, 1), (1, 0)]
NG = 8192
BLOCKS = 16
SPAN = NG // BLOCKS
SLOTS = 320
WIDTH = 384
BOTH = 2 * SLOTS // LANES
LINES = STEPS * BOTH
ELEMS = LINES * BLOCKS
NAMED = 1 << 20
REACH=12
KEPT=2*REACH+1
HALF=GRID//2
PAIR=GRID*GRID*2//LANES
ROWS=GRID**3//LANES
WIDE=16
BACK=16
SLOT=32
PAD_ROWS=40*PAIR


def exchange(x, axis):
    return lax.all_to_all(x, axis, split_axis=0, concat_axis=0, tiled=True)


def rows_kernel(flat, out, rows):
    done = ROWS // 32 * 32
    for at in range(0, done, 32):
        part = flat[:, at * LANES : (at + 32) * LANES].astype(jnp.float32)
        rows[at : at + 32, :] = part.reshape(32, LANES)
    part = flat[:, done * LANES :].astype(jnp.float32)
    rows[done:ROWS, :] = part.reshape(ROWS - done, LANES)
    rows[ROWS:, :] = jnp.zeros((32 * CHUNK - ROWS, LANES), jnp.float32)
    out[...] = rows[...].astype(jnp.bfloat16)


def in_rows(flat):
    return pl.pallas_call(
        rows_kernel,
        out_shape=jax.ShapeDtypeStruct((32 * CHUNK, LANES), jnp.bfloat16),
        in_specs=[pl.BlockSpec(memory_space=pltpu.VMEM)],
        out_specs=pl.BlockSpec(memory_space=pltpu.VMEM),
        scratch_shapes=[pltpu.VMEM((32 * CHUNK, LANES), jnp.float32)],
        cost_estimate=pl.CostEstimate(flops=0, bytes_accessed=4 * 2**20, transcendentals=0),
        compiler_params=pltpu.CompilerParams(vmem_limit_bytes=32 * 2**20),
    )(flat)


def from_owners(shard, owner):
    parts = exchange(in_rows(shard).reshape(32, CHUNK, LANES), PLANE)
    parts = [lax.dynamic_index_in_dim(parts, owner[s] & 31, 0, False) for s in range(STEPS)]
    parts = lax.all_gather(jnp.concatenate(parts, axis=0), "z", axis=0, tiled=True)
    parts = parts.reshape(16, STEPS, CHUNK, LANES)
    parts = [lax.dynamic_index_in_dim(parts[:, s], owner[s] >> 5, 0, False) for s in range(STEPS)]
    parts = jnp.concatenate(parts, axis=0)
    parts = exchange(jnp.broadcast_to(parts[None], (16,) + parts.shape), TILE)
    return parts, lax.ppermute(parts, "c", SWAP)


def split(x):
    high=x.astype(jnp.bfloat16)
    return high,(x-high.astype(jnp.float32)).astype(jnp.bfloat16)

def split_np(x):
    h=x.astype(ml_dtypes.bfloat16)
    return h,(x-h.astype(np.float64)).astype(ml_dtypes.bfloat16)

def tables():
    point=np.arange(GRID)
    def cs(freq):
        ang=2*math.pi*((freq[:,None]*point[None,:])%GRID)/GRID
        return np.cos(ang),np.sin(ang)
    c,s=cs(np.arange(REACH+1))
    t=np.zeros((2,WIDE,2,40))
    t[0,:REACH+1,0,:HALF]=c[:,0::2]; t[0,:REACH+1,1,:HALF]=c[:,1::2]
    t[1,:REACH+1,0,:HALF]=-s[:,0::2]; t[1,:REACH+1,1,:HALF]=-s[:,1::2]
    t=t.reshape(2*WIDE,80)
    h,l=split_np(t)
    first=np.concatenate([h,h,l],1)
    c,s=cs(np.arange(-REACH,REACH+1))
    w=np.zeros((2,LANES,4,SLOT))
    w[0,:GRID,0,:KEPT]=c.T; w[0,:GRID,1,:KEPT]=-s.T
    w[1,:GRID,0,:KEPT]=s.T; w[1,:GRID,1,:KEPT]=c.T
    w[:,:,2]=w[:,:,1]; w[:,:,3]=-w[:,:,0]
    w=w.reshape(2*LANES,LANES)
    h,l=split_np(w)
    third=np.concatenate([h,l],1)
    u=np.zeros((2,2,BACK,GRID))
    u[0,0,:REACH+1]=c[0::2]; u[0,1,:REACH]=c[1::2]
    u[1,0,:REACH+1]=s[0::2]; u[1,1,:REACH]=s[1::2]
    u=u.reshape(4*BACK,GRID)
    h,l=split_np(u)
    second=np.concatenate([h,h,l],1)
    return first,second,third

def dft_kernel(core, owner, val_energy, cond_energy, same, other, cond, first, second, third, places, out, vals, held, mixed, spread, lined):
    f32=jnp.float32; bf=jnp.bfloat16
    for s in range(STEPS):
        vals[s, 32 * CHUNK :, :] = jnp.zeros((PAD_ROWS - 32 * CHUNK, LANES), f32)
        for t in range(16):
            for psi, side in ((same, core[0]), (other, 1 - core[0])):
                here = pl.ds(pl.multiple_of((2 * t + side) * CHUNK, CHUNK), CHUNK)
                band = psi[t, s * CHUNK : (s + 1) * CHUNK, :].astype(f32)
                vals[s, here, :] = band * cond[here, :].astype(f32)
    left=lax.broadcasted_iota(jnp.int32,(40,LANES),1)<LANES//2
    table=first[...]
    zero=jnp.zeros((40,LANES),f32)
    rolled=[pltpu.roll(vals[s,pl.ds(40,40,stride=PAIR),:],LANES//2,1) for s in range(STEPS)]
    for t in range(41):
        cols=[]
        for s in range(STEPS):
            even=vals[s,pl.ds(t,40,stride=PAIR),:]
            here=rolled[s]
            ahead=pltpu.roll(vals[s,pl.ds(41+t,40,stride=PAIR),:],LANES//2,1) if t<40 else zero
            rolled[s]=ahead
            odd=jnp.where(left,here,ahead)
            x=jnp.concatenate([even,odd],0)
            h=x.astype(bf).astype(f32)
            cols.append(jnp.concatenate([h,x-h,h],0).astype(bf))
        y=jnp.dot(table,jnp.concatenate(cols,1),preferred_element_type=f32)
        for s in range(STEPS):
            held[s,:,t*LANES:(t+1)*LANES]=y[:,s*LANES:(s+1)*LANES]
    w=third[...]
    group=8
    for j0 in range(0,GRID,group):
        parts=[[],[]]
        for j in range(j0,j0+group):
            for s in range(STEPS):
                x=held[s,:,j*GRID:j*GRID+LANES]
                parts[0].append(x[:WIDE]); parts[1].append(x[WIDE:])
        x=jnp.concatenate([jnp.concatenate(parts[0],0),jnp.concatenate(parts[1],0)],1)
        h,l=split(x)
        y=jnp.dot(h,w,preferred_element_type=f32)
        z=jnp.dot(l,w[:,:LANES],preferred_element_type=f32)
        mixed[j0*32:(j0+group)*32,:]=y[:,:LANES]+y[:,LANES:]+z
    table=second[...]
    near = lax.broadcasted_iota(jnp.int32, (BACK, LANES), 1) < LANES // 2
    factors = []
    for s in range(STEPS):
        gap = jnp.full((BACK, LANES), cond_energy[0] - val_energy[owner[s]], f32)
        factors.append(jnp.sqrt(4.0 / gap) / math.sqrt(GRID**3))
    for i in range(REACH+1):
        cols=[]
        for s in range(STEPS):
            x=mixed[pl.ds(s*WIDE+i,GRID,stride=32),:]
            h=x.astype(bf).astype(f32)
            cols.append(jnp.concatenate([h,x-h,h],0).astype(bf))
        y=jnp.dot(table,jnp.concatenate(cols,1),preferred_element_type=f32)
        for s in range(STEPS):
            z=y[:,s*LANES:(s+1)*LANES]
            r=z[:2*BACK]+pltpu.roll(z[2*BACK:],LANES//2,1)
            r=jnp.where(near,r[:BACK],pltpu.roll(r[BACK:],LANES//2,1))*factors[s]
            spread[i*BACK:(i+1)*BACK, s*LANES:(s+1)*LANES]=r
    rows = (REACH + 1) * BACK
    data = spread[...].T.astype(bf)
    at = lax.broadcasted_iota(jnp.int32, (rows, WIDTH), 0)
    slot = lax.broadcasted_iota(jnp.int32, (SLOT, WIDTH), 0)
    gap = jnp.zeros((STEPS, 2 * LANES), f32)
    for b in range(BLOCKS):
        place = places[b : b + 1, :]
        hot = jnp.where(at == (place >> 7), 1.0, 0.0).astype(bf)
        y = jnp.dot(data, hot, preferred_element_type=f32)
        keep = slot == (place & (SLOT - 1))
        even = (place & (LANES // 2)) == 0
        got = []
        for s in range(STEPS):
            half = y[s * LANES : (s + 1) * LANES]
            half = jnp.where(even, half[: LANES // 2], half[LANES // 2 :])
            for part in (half[:SLOT], half[SLOT:]):
                got.append(jnp.sum(jnp.where(keep, part, 0.0), 0, keepdims=True))
        real = jnp.concatenate([jnp.concatenate(got[0::2], 0), gap], 1)
        imag = pltpu.roll(jnp.concatenate(got[1::2], 0), WIDTH - SLOTS, 1)
        both = real + jnp.concatenate([gap, imag], 1)
        for s in range(STEPS):
            for n in range(BOTH):
                at_line = (s * BOTH + n) * BLOCKS + b
                lined[at_line : at_line + 1, :] = both[s : s + 1, n * LANES : (n + 1) * LANES]
    out[...] = lined[...].astype(bf)


def turn_kernel(block, gathered, out, rows):
    rows[...] = gathered[...].astype(jnp.float32)
    for b in range(BLOCKS):
        for line in range(LINES):
            s, n = line // BOTH, line % BOTH
            got = rows[pl.ds(line * BLOCKS + b, 16, stride=ELEMS), :]
            to = (n * STEPS + s) * 16
            out[b, to : to + 16, :] = got.astype(jnp.bfloat16)
    chosen = out[block[0], :ELEMS, :]
    for b in range(BLOCKS):
        out[b, ELEMS:, :] = chosen


def turn(block, gathered):
    vm = pl.BlockSpec(memory_space=pltpu.VMEM)
    return pl.pallas_call(
        turn_kernel,
        out_shape=jax.ShapeDtypeStruct((BLOCKS, 2 * ELEMS, LANES), jnp.bfloat16),
        in_specs=[pl.BlockSpec(memory_space=pltpu.SMEM), vm],
        out_specs=vm,
        scratch_shapes=[pltpu.VMEM((16 * ELEMS, LANES), jnp.float32)],
        compiler_params=pltpu.CompilerParams(vmem_limit_bytes=32 * 2**20),
    )(block, gathered)


def frequency_id(i, j, k):
    j = j + REACH
    return (i * BACK + (j >> 1)) * LANES + (j & 1) * (LANES // 2) + k + REACH


def layout():
    axis = np.arange(-REACH, REACH + 1)
    grid = np.stack(np.meshgrid(axis, axis, axis, indexing="ij"), -1).reshape(-1, 3)
    length = (grid**2).sum(1)
    fixed = np.full((BLOCKS, WIDTH), -1)
    kind = np.zeros((BLOCKS, WIDTH), np.int32)
    target = np.full((BLOCKS, SPAN), -1)
    own = np.full((BLOCKS, WIDTH), -5)
    begin = [0] * BLOCKS
    shells = [[] for _ in range(BLOCKS)]
    ends = [0] * BLOCKS
    at = 0
    for value in np.unique(length):
        if at >= NG:
            break
        shell = grid[length == value]
        stop = min(at + len(shell), NG)
        for b in range(at // SPAN, (stop - 1) // SPAN + 1):
            low, high = max(at, b * SPAN), min(stop, b * SPAN + SPAN)
            if high - low == len(shell) or 2 * (high - low) > len(shell):
                i, j, k = shell.T
                front = (i > 0) | ((i == 0) & ((j > 0) | ((j == 0) & (k >= 0))))
                i, j, k = shell[front].T
                shells[b].append(frequency_id(i, j, k))
            elif low == b * SPAN:
                begin[b] = high - low
            else:
                assert high == b * SPAN + SPAN
                ends[b] = high - low
        at = stop
    for b in range(BLOCKS):
        known = np.concatenate(shells[b])
        assert begin[b] + len(known) + ends[b] <= SLOTS
        fixed[b, begin[b] : begin[b] + len(known)] = known
        own[b, begin[b] : begin[b] + len(known)] = known
        kind[b, : begin[b]] = 1
        kind[b, SLOTS - ends[b] : SLOTS] = 2
        target[b, : begin[b]] = NAMED + np.arange(begin[b])
        target[b, SPAN - ends[b] :] = NAMED + np.arange(SLOTS - ends[b], SLOTS)
        places = np.arange(WIDTH)
        own[b] = np.where(kind[b] > 0, NAMED + places, own[b])
    columns = np.full((2, WIDTH, LANES), -5.0, np.float32)
    columns[0, :, :BLOCKS] = own.T
    columns[1, WIDTH - SLOTS :, :BLOCKS] = own.T[:SLOTS]
    return fixed.astype(np.int32), kind, target.astype(np.int32), columns


def frequencies(g_index):
    fixed, kind, target, _ = layout()
    g = g_index.reshape(BLOCKS, SPAN)
    half = GRID // 2
    i, j, k = g // (GRID * GRID), g // GRID % GRID, g % GRID
    i, j, k = [jnp.where(n < half, n, n - GRID) for n in (i, j, k)]
    front = (i > 0) | ((i == 0) & ((j > 0) | ((j == 0) & (k >= 0))))
    sign = jnp.where(front, 1, -1)
    ids = frequency_id(i * sign, j * sign, k * sign)
    first = ids[:, :WIDTH]
    last = jnp.pad(ids[:, SPAN - SLOTS :], ((0, 0), (0, WIDTH - SLOTS)))
    places = jnp.where(kind == 1, first, jnp.where(kind == 2, last, fixed))
    names = jnp.where(target >= 0, target, ids)
    return places, names.astype(jnp.float32), sign.astype(jnp.float32)


def pairs(psi, cond, core, owner, val_energy, cond_energy, places):
    first, second, third = [jnp.asarray(table) for table in (tables())]
    vm = pl.BlockSpec(memory_space=pltpu.VMEM)
    return pl.pallas_call(
        dft_kernel,
        out_shape=jax.ShapeDtypeStruct((ELEMS, LANES), jnp.bfloat16),
        in_specs=[pl.BlockSpec(memory_space=pltpu.SMEM)] * 4 + [vm] * 7,
        out_specs=vm,
        scratch_shapes=[
            pltpu.VMEM((STEPS, PAD_ROWS, LANES), jnp.float32),
            pltpu.VMEM((STEPS, 2 * WIDE, 41 * LANES), jnp.float32),
            pltpu.VMEM((GRID * 32, LANES), jnp.float32),
            pltpu.VMEM(((REACH + 1) * BACK, STEPS * LANES), jnp.float32),
            pltpu.VMEM((ELEMS, LANES), jnp.float32),
        ],
        compiler_params=pltpu.CompilerParams(vmem_limit_bytes=48 * 2**20),
    )(core, owner, val_energy, cond_energy, *psi, cond, first, second, third, places)


def sums_kernel(me, elems, names, signs, columns, out):
    f32, bf = jnp.float32, jnp.bfloat16
    z, m, yl = [me[n] for n in range(3)]
    half = SPAN // 2

    def spread(block, side):
        name, sign = names[pl.ds(block, 1), :], signs[pl.ds(block, 1), :]
        if side is not None:
            name, sign = [jnp.where(side == 0, x[:, :half], x[:, half:]) for x in (name, sign)]
        chosen = lax.broadcasted_iota(jnp.int32, (WIDTH, LANES), 1) == block
        place = [jnp.sum(jnp.where(chosen, columns[p], 0.0), 1, keepdims=True) for p in range(2)]
        real = jnp.where(place[0] == name, 1.0, 0.0).astype(bf)
        return real, jnp.where(place[1] == name, sign, 0.0).astype(bf)

    def lanes(n):
        return elems[:, n * 32 : (n + 1) * 32, :].reshape(-1, LANES)

    def widened(tiles, hot):
        real = jnp.dot(jnp.concatenate(tiles[:3], 1), hot[0], preferred_element_type=f32)
        imag = jnp.dot(jnp.concatenate(tiles[2:], 1), hot[1], preferred_element_type=f32)
        return real.astype(bf), imag.astype(bf)

    left = widened([lanes(BOTH + n) for n in range(BOTH)], spread(z, yl))
    right = widened([lanes(n) for n in range(BOTH)], spread(m, None))
    over = (((0,), (0,)), ((), ()))
    total = lax.dot_general(left[0], right[0], over, preferred_element_type=f32)
    total += lax.dot_general(left[1], right[1], over, preferred_element_type=f32)
    out[...] = (total * (-1.0 / math.sqrt(STEPS * 512))).astype(out.dtype)


def sums(me, elems, names, signs, dtype):
    vm = pl.BlockSpec(memory_space=pltpu.VMEM)
    return pl.pallas_call(
        sums_kernel,
        out_shape=jax.ShapeDtypeStruct((SPAN // 2, SPAN), dtype),
        in_specs=[pl.BlockSpec(memory_space=pltpu.SMEM)] + [vm] * 4,
        out_specs=vm,
        cost_estimate=pl.CostEstimate(flops=10**9, bytes_accessed=2 * 2**20, transcendentals=0),
        compiler_params=pltpu.CompilerParams(vmem_limit_bytes=48 * 2**20),
    )(me, elems, names, signs, jnp.asarray(layout()[3]))


def body(valence, conduction, val_energy, cond_energy, owner, g_index):
    psi = from_owners(valence, owner)
    cond = in_rows(conduction)
    places, names, signs = frequencies(g_index)
    core = lax.axis_index("c").astype(jnp.int32)
    elems = pairs(psi, cond, core[None], owner, val_energy, cond_energy, places)

    elems = lax.all_gather(elems, "z", axis=0, tiled=True)
    place = [lax.axis_index(a) for a in ("z", COL, "yl")]
    me = jnp.stack(place).astype(jnp.int32)
    partner = jnp.stack(place[:2] + [1 - place[2]]).astype(jnp.int32)
    elems = exchange(turn(me, elems), COL)
    away = sums(partner, elems, names, signs, jnp.bfloat16)
    away = lax.ppermute(away, "yl", SWAP)
    return sums(me, elems, names, signs, jnp.float32) + away.astype(jnp.float32)


def solution(mesh):
    every = P(AXES)
    return jax.shard_map(
        body,
        mesh=Mesh(mesh.devices.reshape(SIZES), AXES),
        in_specs=(P(AXES, None), P(AXES, None), P(), every, P(), P()),
        out_specs=P(ROW, COL),
        check_vma=False,
    )
```

```python
import functools
import math

import jax
import jax.numpy as jnp
import ml_dtypes
import numpy as np
from jax import lax
from jax.experimental import pallas as pl
from jax.experimental.pallas import tpu as pltpu
from jax.sharding import Mesh, PartitionSpec as P

GRID = 72
STEPS = 2
AXES = ("z", "yl", "x", "yh", "c")
SIZES = (16, 2, 4, 2, 2)
ROW = ("z", "yl")
COL = ("x", "yh", "c")
PLANE = ("yl", "x", "yh", "c")
TILE = ("yl", "x", "yh")
QUAD = ("x", "yh")
LANES = 128
PIECE = 6
CHUNK = 16 * PIECE
SWAP = [(0, 1), (1, 0)]
NG = 8192
BLOCKS = 16
SPAN = NG // BLOCKS
SLOTS = 320
WIDTH = 384
BOTH = 2 * SLOTS // LANES
LINES = STEPS * BOTH
ELEMS = LINES * BLOCKS
NAMED = 1 << 20
REACH=12
KEPT=2*REACH+1
HALF=GRID//2
PAIR=GRID*GRID*2//LANES
ROWS=GRID**3//LANES
WIDE=16
BACK=16
SLOT=32
PAD_ROWS=40*PAIR


def exchange(x, axis):
    return lax.all_to_all(x, axis, split_axis=0, concat_axis=0, tiled=True)


def rows_kernel(flat, out, rows):
    done = ROWS // 32 * 32
    for at in range(0, done, 32):
        part = flat[:, at * LANES : (at + 32) * LANES].astype(jnp.float32)
        rows[at : at + 32, :] = part.reshape(32, LANES)
    part = flat[:, done * LANES :].astype(jnp.float32)
    rows[done:ROWS, :] = part.reshape(ROWS - done, LANES)
    rows[ROWS:, :] = jnp.zeros((32 * CHUNK - ROWS, LANES), jnp.float32)
    out[...] = rows[...].astype(jnp.bfloat16)


def in_rows(flat):
    return pl.pallas_call(
        rows_kernel,
        out_shape=jax.ShapeDtypeStruct((32 * CHUNK, LANES), jnp.bfloat16),
        in_specs=[pl.BlockSpec(memory_space=pltpu.VMEM)],
        out_specs=pl.BlockSpec(memory_space=pltpu.VMEM),
        scratch_shapes=[pltpu.VMEM((32 * CHUNK, LANES), jnp.float32)],
        cost_estimate=pl.CostEstimate(flops=0, bytes_accessed=4 * 2**20, transcendentals=0),
        compiler_params=pltpu.CompilerParams(vmem_limit_bytes=32 * 2**20),
    )(flat)


def from_owners(shard, owner, late):
    parts = exchange(in_rows(shard).reshape(32, CHUNK, LANES), PLANE)
    parts = [lax.dynamic_index_in_dim(parts, owner[s] & 31, 0, False) for s in range(STEPS)]
    parts = lax.all_gather(jnp.concatenate(parts, axis=0), "z", axis=0, tiled=True)
    parts = parts.reshape(16, STEPS, CHUNK, LANES)
    parts = [lax.dynamic_index_in_dim(parts[:, s], owner[s] >> 5, 0, False) for s in range(STEPS)]
    parts = jnp.concatenate(parts, axis=0)
    parts = exchange(jnp.broadcast_to(parts[None], (16,) + parts.shape), TILE)
    parts, late = lax.optimization_barrier((parts, late))
    return (parts, lax.ppermute(parts, "c", SWAP)), late


def split(x):
    high=x.astype(jnp.bfloat16)
    return high,(x-high.astype(jnp.float32)).astype(jnp.bfloat16)

def split_np(x):
    h=x.astype(ml_dtypes.bfloat16)
    return h,(x-h.astype(np.float64)).astype(ml_dtypes.bfloat16)

def tables():
    point=np.arange(GRID)
    def cs(freq):
        ang=2*math.pi*((freq[:,None]*point[None,:])%GRID)/GRID
        return np.cos(ang),np.sin(ang)
    c,s=cs(np.arange(REACH+1))
    t=np.zeros((2,WIDE,2,40))
    t[0,:REACH+1,0,:HALF]=c[:,0::2]; t[0,:REACH+1,1,:HALF]=c[:,1::2]
    t[1,:REACH+1,0,:HALF]=-s[:,0::2]; t[1,:REACH+1,1,:HALF]=-s[:,1::2]
    t=t.reshape(2*WIDE,80)
    h,l=split_np(t)
    first=np.concatenate([h,h,l],1)
    c,s=cs(np.arange(-REACH,REACH+1))
    w=np.zeros((2,LANES,4,SLOT))
    w[0,:GRID,0,:KEPT]=c.T; w[0,:GRID,1,:KEPT]=-s.T
    w[1,:GRID,0,:KEPT]=s.T; w[1,:GRID,1,:KEPT]=c.T
    w[:,:,2]=w[:,:,1]; w[:,:,3]=-w[:,:,0]
    w=w.reshape(2*LANES,LANES)
    h,l=split_np(w)
    third=np.concatenate([h,l],1)
    u=np.zeros((2,2,BACK,GRID))
    u[0,0,:REACH+1]=c[0::2]; u[0,1,:REACH]=c[1::2]
    u[1,0,:REACH+1]=s[0::2]; u[1,1,:REACH]=s[1::2]
    u=u.reshape(4*BACK,GRID)
    h,l=split_np(u)
    second=np.concatenate([h,h,l],1)
    return first,second,third

def dft_kernel(owner, val_energy, cond_energy, same, other, cond, first, second, third, places, out, vals, held, mixed, spread, lined):
    f32=jnp.float32; bf=jnp.bfloat16
    core = lax.axis_index("c")
    for s in range(STEPS):
        vals[s, 32 * CHUNK :, :] = jnp.zeros((PAD_ROWS - 32 * CHUNK, LANES), f32)
        for t in range(16):
            for psi, side in ((same, core), (other, 1 - core)):
                here = pl.ds(pl.multiple_of((2 * t + side) * CHUNK, CHUNK), CHUNK)
                band = psi[t, s * CHUNK : (s + 1) * CHUNK, :].astype(f32)
                vals[s, here, :] = band * cond[here, :].astype(f32)
    left=lax.broadcasted_iota(jnp.int32,(40,LANES),1)<LANES//2
    table=first[...]
    zero=jnp.zeros((40,LANES),f32)
    rolled=[pltpu.roll(vals[s,pl.ds(40,40,stride=PAIR),:],LANES//2,1) for s in range(STEPS)]
    for t in range(41):
        cols=[]
        for s in range(STEPS):
            even=vals[s,pl.ds(t,40,stride=PAIR),:]
            here=rolled[s]
            ahead=pltpu.roll(vals[s,pl.ds(41+t,40,stride=PAIR),:],LANES//2,1) if t<40 else zero
            rolled[s]=ahead
            odd=jnp.where(left,here,ahead)
            x=jnp.concatenate([even,odd],0)
            h=x.astype(bf).astype(f32)
            cols.append(jnp.concatenate([h,x-h,h],0).astype(bf))
        y=jnp.dot(table,jnp.concatenate(cols,1),preferred_element_type=f32)
        for s in range(STEPS):
            held[s,:,t*LANES:(t+1)*LANES]=y[:,s*LANES:(s+1)*LANES]
    w=third[...]
    group=8
    for j0 in range(0,GRID,group):
        parts=[[],[]]
        for j in range(j0,j0+group):
            for s in range(STEPS):
                x=held[s,:,j*GRID:j*GRID+LANES]
                parts[0].append(x[:WIDE]); parts[1].append(x[WIDE:])
        x=jnp.concatenate([jnp.concatenate(parts[0],0),jnp.concatenate(parts[1],0)],1)
        h,l=split(x)
        y=jnp.dot(h,w,preferred_element_type=f32)
        z=jnp.dot(l,w[:,:LANES],preferred_element_type=f32)
        mixed[j0*32:(j0+group)*32,:]=y[:,:LANES]+y[:,LANES:]+z
    table=second[...]
    near = lax.broadcasted_iota(jnp.int32, (BACK, LANES), 1) < LANES // 2
    factors = []
    for s in range(STEPS):
        gap = jnp.full((BACK, LANES), cond_energy[0] - val_energy[owner[s]], f32)
        factors.append(jnp.sqrt(4.0 / gap) / math.sqrt(GRID**3))
    for i in range(REACH+1):
        cols=[]
        for s in range(STEPS):
            x=mixed[pl.ds(s*WIDE+i,GRID,stride=32),:]
            h=x.astype(bf).astype(f32)
            cols.append(jnp.concatenate([h,x-h,h],0).astype(bf))
        y=jnp.dot(table,jnp.concatenate(cols,1),preferred_element_type=f32)
        for s in range(STEPS):
            z=y[:,s*LANES:(s+1)*LANES]
            r=z[:2*BACK]+pltpu.roll(z[2*BACK:],LANES//2,1)
            r=jnp.where(near,r[:BACK],pltpu.roll(r[BACK:],LANES//2,1))*factors[s]
            spread[i*BACK:(i+1)*BACK, s*LANES:(s+1)*LANES]=r
    rows = (REACH + 1) * BACK
    data = spread[...].T.astype(bf)
    at = lax.broadcasted_iota(jnp.int32, (rows, WIDTH), 0)
    slot = lax.broadcasted_iota(jnp.int32, (SLOT, WIDTH), 0)
    gap = jnp.zeros((STEPS, 2 * LANES), f32)
    for b in range(BLOCKS):
        place = places[b : b + 1, :]
        hot = jnp.where(at == (place >> 7), 1.0, 0.0).astype(bf)
        y = jnp.dot(data, hot, preferred_element_type=f32)
        keep = slot == (place & (SLOT - 1))
        even = (place & (LANES // 2)) == 0
        got = []
        for s in range(STEPS):
            half = y[s * LANES : (s + 1) * LANES]
            half = jnp.where(even, half[: LANES // 2], half[LANES // 2 :])
            for part in (half[:SLOT], half[SLOT:]):
                got.append(jnp.sum(jnp.where(keep, part, 0.0), 0, keepdims=True))
        real = jnp.concatenate([jnp.concatenate(got[0::2], 0), gap], 1)
        imag = pltpu.roll(jnp.concatenate(got[1::2], 0), WIDTH - SLOTS, 1)
        both = real + jnp.concatenate([gap, imag], 1)
        for s in range(STEPS):
            for n in range(BOTH):
                at_line = (s * BOTH + n) * BLOCKS + b
                lined[at_line : at_line + 1, :] = both[s : s + 1, n * LANES : (n + 1) * LANES]
    out[...] = lined[...].astype(bf)


def turn_kernel(gathered, out, rows):
    rows[...] = gathered[...].astype(jnp.float32)
    for b in range(BLOCKS):
        for line in range(LINES):
            s, n = line // BOTH, line % BOTH
            got = rows[pl.ds(line * BLOCKS + b, 16, stride=ELEMS), :]
            to = (n * STEPS + s) * 16
            out[b, to : to + 16, :] = got.astype(jnp.bfloat16)
    chosen = out[lax.axis_index("z"), :ELEMS, :]
    for b in range(BLOCKS):
        out[b, ELEMS:, :] = chosen


def turn(gathered):
    vm = pl.BlockSpec(memory_space=pltpu.VMEM)
    return pl.pallas_call(
        turn_kernel,
        out_shape=jax.ShapeDtypeStruct((BLOCKS, 2 * ELEMS, LANES), jnp.bfloat16),
        in_specs=[vm],
        out_specs=vm,
        scratch_shapes=[pltpu.VMEM((16 * ELEMS, LANES), jnp.float32)],
        compiler_params=pltpu.CompilerParams(vmem_limit_bytes=32 * 2**20),
    )(gathered)


def frequency_id(i, j, k):
    j = j + REACH
    return (i * BACK + (j >> 1)) * LANES + (j & 1) * (LANES // 2) + k + REACH


def layout():
    axis = np.arange(-REACH, REACH + 1)
    grid = np.stack(np.meshgrid(axis, axis, axis, indexing="ij"), -1).reshape(-1, 3)
    length = (grid**2).sum(1)
    fixed = np.full((BLOCKS, WIDTH), -1)
    kind = np.zeros((BLOCKS, WIDTH), np.int32)
    target = np.full((BLOCKS, SPAN), -1)
    own = np.full((BLOCKS, WIDTH), -5)
    begin = [0] * BLOCKS
    shells = [[] for _ in range(BLOCKS)]
    ends = [0] * BLOCKS
    at = 0
    for value in np.unique(length):
        if at >= NG:
            break
        shell = grid[length == value]
        stop = min(at + len(shell), NG)
        for b in range(at // SPAN, (stop - 1) // SPAN + 1):
            low, high = max(at, b * SPAN), min(stop, b * SPAN + SPAN)
            if high - low == len(shell) or 2 * (high - low) > len(shell):
                i, j, k = shell.T
                front = (i > 0) | ((i == 0) & ((j > 0) | ((j == 0) & (k >= 0))))
                i, j, k = shell[front].T
                shells[b].append(frequency_id(i, j, k))
            elif low == b * SPAN:
                begin[b] = high - low
            else:
                assert high == b * SPAN + SPAN
                ends[b] = high - low
        at = stop
    for b in range(BLOCKS):
        known = np.concatenate(shells[b])
        assert begin[b] + len(known) + ends[b] <= SLOTS
        fixed[b, begin[b] : begin[b] + len(known)] = known
        own[b, begin[b] : begin[b] + len(known)] = known
        kind[b, : begin[b]] = 1
        kind[b, SLOTS - ends[b] : SLOTS] = 2
        target[b, : begin[b]] = NAMED + np.arange(begin[b])
        target[b, SPAN - ends[b] :] = NAMED + np.arange(SLOTS - ends[b], SLOTS)
        places = np.arange(WIDTH)
        own[b] = np.where(kind[b] > 0, NAMED + places, own[b])
    columns = np.full((2, WIDTH, LANES), -5.0, np.float32)
    columns[0, :, :BLOCKS] = own.T
    columns[1, WIDTH - SLOTS :, :BLOCKS] = own.T[:SLOTS]
    return fixed.astype(np.int32), kind, target.astype(np.int32), columns


def frequencies(g_index):
    fixed, kind, target, _ = layout()
    g = g_index.reshape(BLOCKS, SPAN)
    half = GRID // 2
    i, j, k = g // (GRID * GRID), g // GRID % GRID, g % GRID
    i, j, k = [jnp.where(n < half, n, n - GRID) for n in (i, j, k)]
    front = (i > 0) | ((i == 0) & ((j > 0) | ((j == 0) & (k >= 0))))
    sign = jnp.where(front, 1, -1)
    ids = frequency_id(i * sign, j * sign, k * sign)
    first = ids[:, :WIDTH]
    last = jnp.pad(ids[:, SPAN - SLOTS :], ((0, 0), (0, WIDTH - SLOTS)))
    places = jnp.where(kind == 1, first, jnp.where(kind == 2, last, fixed))
    names = jnp.where(target >= 0, target, ids)
    return places, names.astype(jnp.float32), sign.astype(jnp.float32)


def pairs(psi, cond, owner, val_energy, cond_energy, places):
    first, second, third = [jnp.asarray(table) for table in (tables())]
    vm = pl.BlockSpec(memory_space=pltpu.VMEM)
    return pl.pallas_call(
        dft_kernel,
        out_shape=jax.ShapeDtypeStruct((ELEMS, LANES), jnp.bfloat16),
        in_specs=[pl.BlockSpec(memory_space=pltpu.SMEM)] * 3 + [vm] * 7,
        out_specs=vm,
        scratch_shapes=[
            pltpu.VMEM((STEPS, PAD_ROWS, LANES), jnp.float32),
            pltpu.VMEM((STEPS, 2 * WIDE, 41 * LANES), jnp.float32),
            pltpu.VMEM((GRID * 32, LANES), jnp.float32),
            pltpu.VMEM(((REACH + 1) * BACK, STEPS * LANES), jnp.float32),
            pltpu.VMEM((ELEMS, LANES), jnp.float32),
        ],
        compiler_params=pltpu.CompilerParams(vmem_limit_bytes=48 * 2**20),
    )(owner, val_energy, cond_energy, *psi, cond, first, second, third, places)


def sums_kernel(partner, elems, names, signs, columns, out):
    f32, bf = jnp.float32, jnp.bfloat16
    z, yl = lax.axis_index("z"), lax.axis_index("yl")
    m = (lax.axis_index("x") * 2 + lax.axis_index("yh")) * 2 + lax.axis_index("c")
    yl = 1 - yl if partner else yl
    half = SPAN // 2

    def spread(block, side):
        name, sign = names[pl.ds(block, 1), :], signs[pl.ds(block, 1), :]
        if side is not None:
            name, sign = [jnp.where(side == 0, x[:, :half], x[:, half:]) for x in (name, sign)]
        chosen = lax.broadcasted_iota(jnp.int32, (WIDTH, LANES), 1) == block
        place = [jnp.sum(jnp.where(chosen, columns[p], 0.0), 1, keepdims=True) for p in range(2)]
        real = jnp.where(place[0] == name, 1.0, 0.0).astype(bf)
        return real, jnp.where(place[1] == name, sign, 0.0).astype(bf)

    def lanes(n):
        return elems[:, n * 32 : (n + 1) * 32, :].reshape(-1, LANES)

    def widened(tiles, hot):
        real = jnp.dot(jnp.concatenate(tiles[:3], 1), hot[0], preferred_element_type=f32)
        imag = jnp.dot(jnp.concatenate(tiles[2:], 1), hot[1], preferred_element_type=f32)
        return real.astype(bf), imag.astype(bf)

    left = widened([lanes(BOTH + n) for n in range(BOTH)], spread(z, yl))
    right = widened([lanes(n) for n in range(BOTH)], spread(m, None))
    over = (((0,), (0,)), ((), ()))
    total = lax.dot_general(left[0], right[0], over, preferred_element_type=f32)
    total += lax.dot_general(left[1], right[1], over, preferred_element_type=f32)
    out[...] = (total * (-1.0 / math.sqrt(STEPS * 512))).astype(out.dtype)


def sums(elems, names, signs, partner):
    vm = pl.BlockSpec(memory_space=pltpu.VMEM)
    return pl.pallas_call(
        functools.partial(sums_kernel, partner),
        out_shape=jax.ShapeDtypeStruct((SPAN // 2, SPAN), jnp.bfloat16 if partner else jnp.float32),
        in_specs=[vm] * 4,
        out_specs=vm,
        cost_estimate=pl.CostEstimate(flops=10**9, bytes_accessed=2 * 2**20, transcendentals=0),
        compiler_params=pltpu.CompilerParams(vmem_limit_bytes=48 * 2**20),
    )(elems, names, signs, jnp.asarray(layout()[3]))


def body(valence, conduction, val_energy, cond_energy, owner, g_index):
    psi, g_index = from_owners(valence, owner, g_index)
    cond = in_rows(conduction)
    places, names, signs = frequencies(g_index)
    elems = pairs(psi, cond, owner, val_energy, cond_energy, places)

    elems = lax.all_gather(elems, "z", axis=0, tiled=True)
    elems = exchange(turn(elems), COL)
    away = lax.ppermute(sums(elems, names, signs, True), "yl", SWAP)
    return sums(elems, names, signs, False) + away.astype(jnp.float32)


def solution(mesh):
    every = P(AXES)
    return jax.shard_map(
        body,
        mesh=Mesh(mesh.devices.reshape(SIZES), AXES),
        in_specs=(P(AXES, None), P(AXES, None), P(), every, P(), P()),
        out_specs=P(ROW, COL),
        check_vma=False,
    )
```

```python
import functools
import math

import jax
import jax.numpy as jnp
import ml_dtypes
import numpy as np
from jax import lax
from jax.experimental import pallas as pl
from jax.experimental.pallas import tpu as pltpu
from jax.sharding import Mesh, PartitionSpec as P

GRID = 72
STEPS = 2
AXES = ("z", "yl", "x", "yh", "c")
SIZES = (16, 2, 4, 2, 2)
ROW = ("z", "yl")
COL = ("x", "yh", "c")
PLANE = ("yl", "x", "yh", "c")
TILE = ("yl", "x", "yh")
QUAD = ("x", "yh")
LANES = 128
PIECE = 6
CHUNK = 16 * PIECE
SWAP = [(0, 1), (1, 0)]
NG = 8192
BLOCKS = 16
SPAN = NG // BLOCKS
SLOTS = 320
WIDTH = 384
BOTH = 2 * SLOTS // LANES
LINES = STEPS * BOTH
ELEMS = LINES * BLOCKS
NAMED = 1 << 20
REACH=12
KEPT=2*REACH+1
HALF=GRID//2
PAIR=GRID*GRID*2//LANES
ROWS=GRID**3//LANES
WIDE=16
BACK=16
SLOT=32
PAD_ROWS=40*PAIR


def exchange(x, axis):
    return lax.all_to_all(x, axis, split_axis=0, concat_axis=0, tiled=True)


def rows_kernel(flat, out, rows):
    done = ROWS // 32 * 32
    for at in range(0, done, 32):
        part = flat[:, at * LANES : (at + 32) * LANES].astype(jnp.float32)
        rows[at : at + 32, :] = part.reshape(32, LANES)
    part = flat[:, done * LANES :].astype(jnp.float32)
    rows[done:ROWS, :] = part.reshape(ROWS - done, LANES)
    rows[ROWS:, :] = jnp.zeros((32 * CHUNK - ROWS, LANES), jnp.float32)
    out[...] = rows[...].astype(jnp.bfloat16)


def in_rows(flat):
    return pl.pallas_call(
        rows_kernel,
        out_shape=jax.ShapeDtypeStruct((32 * CHUNK, LANES), jnp.bfloat16),
        in_specs=[pl.BlockSpec(memory_space=pltpu.VMEM)],
        out_specs=pl.BlockSpec(memory_space=pltpu.VMEM),
        scratch_shapes=[pltpu.VMEM((32 * CHUNK, LANES), jnp.float32)],
        cost_estimate=pl.CostEstimate(flops=0, bytes_accessed=4 * 2**20, transcendentals=0),
        compiler_params=pltpu.CompilerParams(vmem_limit_bytes=32 * 2**20),
    )(flat)


def from_owners(shard, owner, late):
    parts = exchange(in_rows(shard).reshape(32, CHUNK, LANES), PLANE)
    parts = [lax.dynamic_index_in_dim(parts, owner[s] & 31, 0, False) for s in range(STEPS)]
    parts = lax.all_gather(jnp.concatenate(parts, axis=0), "z", axis=0, tiled=True)
    parts = parts.reshape(16, STEPS, CHUNK, LANES)
    parts = [lax.dynamic_index_in_dim(parts[:, s], owner[s] >> 5, 0, False) for s in range(STEPS)]
    parts = jnp.concatenate(parts, axis=0)
    parts = exchange(jnp.broadcast_to(parts[None], (16,) + parts.shape), TILE)
    parts, late = lax.optimization_barrier((parts, late))
    return (parts, lax.ppermute(parts, "c", SWAP)), late


def split(x):
    high=x.astype(jnp.bfloat16)
    return high,(x-high.astype(jnp.float32)).astype(jnp.bfloat16)

def split_np(x):
    h=x.astype(ml_dtypes.bfloat16)
    return h,(x-h.astype(np.float64)).astype(ml_dtypes.bfloat16)

def tables():
    point=np.arange(GRID)
    def cs(freq):
        ang=2*math.pi*((freq[:,None]*point[None,:])%GRID)/GRID
        return np.cos(ang),np.sin(ang)
    c,s=cs(np.arange(REACH+1))
    t=np.zeros((2,WIDE,2,40))
    t[0,:REACH+1,0,:HALF]=c[:,0::2]; t[0,:REACH+1,1,:HALF]=c[:,1::2]
    t[1,:REACH+1,0,:HALF]=-s[:,0::2]; t[1,:REACH+1,1,:HALF]=-s[:,1::2]
    t=t.reshape(2*WIDE,80)
    h,l=split_np(t)
    first=np.concatenate([h,h,l],1)
    c,s=cs(np.arange(-REACH,REACH+1))
    w=np.zeros((2,LANES,4,SLOT))
    w[0,:GRID,0,:KEPT]=c.T; w[0,:GRID,1,:KEPT]=-s.T
    w[1,:GRID,0,:KEPT]=s.T; w[1,:GRID,1,:KEPT]=c.T
    w[:,:,2]=w[:,:,1]; w[:,:,3]=-w[:,:,0]
    w=w.reshape(2*LANES,LANES)
    h,l=split_np(w)
    third=np.concatenate([h,l],1)
    u=np.zeros((2,2,BACK,GRID))
    u[0,0,:REACH+1]=c[0::2]; u[0,1,:REACH]=c[1::2]
    u[1,0,:REACH+1]=s[0::2]; u[1,1,:REACH]=s[1::2]
    u=u.reshape(4*BACK,GRID)
    h,l=split_np(u)
    second=np.concatenate([h,h,l],1)
    return first,second,third

def dft_kernel(owner, val_energy, cond_energy, same, other, cond, first, second, third, places, out, vals, held, mixed, spread, lined):
    f32=jnp.float32; bf=jnp.bfloat16
    core = lax.axis_index("c")
    for s in range(STEPS):
        vals[s, 32 * CHUNK :, :] = jnp.zeros((PAD_ROWS - 32 * CHUNK, LANES), f32)
        for t in range(16):
            for psi, side in ((same, core), (other, 1 - core)):
                here = pl.ds(pl.multiple_of((2 * t + side) * CHUNK, CHUNK), CHUNK)
                band = psi[t, s * CHUNK : (s + 1) * CHUNK, :].astype(f32)
                vals[s, here, :] = band * cond[here, :].astype(f32)
    left=lax.broadcasted_iota(jnp.int32,(40,LANES),1)<LANES//2
    table=first[...]
    zero=jnp.zeros((40,LANES),f32)
    rolled=[pltpu.roll(vals[s,pl.ds(40,40,stride=PAIR),:],LANES//2,1) for s in range(STEPS)]
    for t in range(41):
        cols=[]
        for s in range(STEPS):
            even=vals[s,pl.ds(t,40,stride=PAIR),:]
            here=rolled[s]
            ahead=pltpu.roll(vals[s,pl.ds(41+t,40,stride=PAIR),:],LANES//2,1) if t<40 else zero
            rolled[s]=ahead
            odd=jnp.where(left,here,ahead)
            x=jnp.concatenate([even,odd],0)
            h=x.astype(bf).astype(f32)
            cols.append(jnp.concatenate([h,x-h,h],0).astype(bf))
        y=jnp.dot(table,jnp.concatenate(cols,1),preferred_element_type=f32)
        for s in range(STEPS):
            held[s,:,t*LANES:(t+1)*LANES]=y[:,s*LANES:(s+1)*LANES]
    w=third[...]
    group=GRID
    for j0 in range(0,GRID,group):
        parts=[[],[]]
        for j in range(j0,j0+group):
            for s in range(STEPS):
                x=held[s,:,j*GRID:j*GRID+LANES]
                parts[0].append(x[:WIDE]); parts[1].append(x[WIDE:])
        x=jnp.concatenate([jnp.concatenate(parts[0],0),jnp.concatenate(parts[1],0)],1)
        h,l=split(x)
        y=jnp.dot(h,w,preferred_element_type=f32)
        z=jnp.dot(l,w[:,:LANES],preferred_element_type=f32)
        mixed[j0*32:(j0+group)*32,:]=y[:,:LANES]+y[:,LANES:]+z
    table=second[...]
    near = lax.broadcasted_iota(jnp.int32, (BACK, LANES), 1) < LANES // 2
    factors = []
    for s in range(STEPS):
        gap = jnp.full((BACK, LANES), cond_energy[0] - val_energy[owner[s]], f32)
        factors.append(jnp.sqrt(4.0 / gap) / math.sqrt(GRID**3))
    for i in range(REACH+1):
        cols=[]
        for s in range(STEPS):
            x=mixed[pl.ds(s*WIDE+i,GRID,stride=32),:]
            h=x.astype(bf).astype(f32)
            cols.append(jnp.concatenate([h,x-h,h],0).astype(bf))
        y=jnp.dot(table,jnp.concatenate(cols,1),preferred_element_type=f32)
        for s in range(STEPS):
            z=y[:,s*LANES:(s+1)*LANES]
            r=z[:2*BACK]+pltpu.roll(z[2*BACK:],LANES//2,1)
            r=jnp.where(near,r[:BACK],pltpu.roll(r[BACK:],LANES//2,1))*factors[s]
            spread[i*BACK:(i+1)*BACK, s*LANES:(s+1)*LANES]=r
    rows = (REACH + 1) * BACK
    data = spread[...].T.astype(bf)
    at = lax.broadcasted_iota(jnp.int32, (rows, WIDTH), 0)
    slot = lax.broadcasted_iota(jnp.int32, (SLOT, WIDTH), 0)
    gap = jnp.zeros((STEPS, 2 * LANES), f32)
    for b in range(BLOCKS):
        place = places[b : b + 1, :]
        hot = jnp.where(at == (place >> 7), 1.0, 0.0).astype(bf)
        y = jnp.dot(data, hot, preferred_element_type=f32)
        keep = slot == (place & (SLOT - 1))
        even = (place & (LANES // 2)) == 0
        got = []
        for s in range(STEPS):
            half = y[s * LANES : (s + 1) * LANES]
            half = jnp.where(even, half[: LANES // 2], half[LANES // 2 :])
            for part in (half[:SLOT], half[SLOT:]):
                got.append(jnp.sum(jnp.where(keep, part, 0.0), 0, keepdims=True))
        real = jnp.concatenate([jnp.concatenate(got[0::2], 0), gap], 1)
        imag = pltpu.roll(jnp.concatenate(got[1::2], 0), WIDTH - SLOTS, 1)
        both = real + jnp.concatenate([gap, imag], 1)
        for s in range(STEPS):
            for n in range(BOTH):
                at_line = (s * BOTH + n) * BLOCKS + b
                lined[at_line : at_line + 1, :] = both[s : s + 1, n * LANES : (n + 1) * LANES]
    out[...] = lined[...].astype(bf)


def turn_kernel(gathered, out, rows):
    rows[...] = gathered[...].astype(jnp.float32)
    for b in range(BLOCKS):
        for line in range(LINES):
            s, n = line // BOTH, line % BOTH
            got = rows[pl.ds(line * BLOCKS + b, 16, stride=ELEMS), :]
            to = (n * STEPS + s) * 16
            out[b, to : to + 16, :] = got.astype(jnp.bfloat16)
    chosen = out[lax.axis_index("z"), :ELEMS, :]
    for b in range(BLOCKS):
        out[b, ELEMS:, :] = chosen


def turn(gathered):
    vm = pl.BlockSpec(memory_space=pltpu.VMEM)
    return pl.pallas_call(
        turn_kernel,
        out_shape=jax.ShapeDtypeStruct((BLOCKS, 2 * ELEMS, LANES), jnp.bfloat16),
        in_specs=[vm],
        out_specs=vm,
        scratch_shapes=[pltpu.VMEM((16 * ELEMS, LANES), jnp.float32)],
        compiler_params=pltpu.CompilerParams(vmem_limit_bytes=32 * 2**20),
    )(gathered)


def frequency_id(i, j, k):
    j = j + REACH
    return (i * BACK + (j >> 1)) * LANES + (j & 1) * (LANES // 2) + k + REACH


def layout():
    axis = np.arange(-REACH, REACH + 1)
    grid = np.stack(np.meshgrid(axis, axis, axis, indexing="ij"), -1).reshape(-1, 3)
    length = (grid**2).sum(1)
    fixed = np.full((BLOCKS, WIDTH), -1)
    kind = np.zeros((BLOCKS, WIDTH), np.int32)
    target = np.full((BLOCKS, SPAN), -1)
    own = np.full((BLOCKS, WIDTH), -5)
    begin = [0] * BLOCKS
    shells = [[] for _ in range(BLOCKS)]
    ends = [0] * BLOCKS
    at = 0
    for value in np.unique(length):
        if at >= NG:
            break
        shell = grid[length == value]
        stop = min(at + len(shell), NG)
        for b in range(at // SPAN, (stop - 1) // SPAN + 1):
            low, high = max(at, b * SPAN), min(stop, b * SPAN + SPAN)
            if high - low == len(shell) or 2 * (high - low) > len(shell):
                i, j, k = shell.T
                front = (i > 0) | ((i == 0) & ((j > 0) | ((j == 0) & (k >= 0))))
                i, j, k = shell[front].T
                shells[b].append(frequency_id(i, j, k))
            elif low == b * SPAN:
                begin[b] = high - low
            else:
                assert high == b * SPAN + SPAN
                ends[b] = high - low
        at = stop
    for b in range(BLOCKS):
        known = np.concatenate(shells[b])
        assert begin[b] + len(known) + ends[b] <= SLOTS
        fixed[b, begin[b] : begin[b] + len(known)] = known
        own[b, begin[b] : begin[b] + len(known)] = known
        kind[b, : begin[b]] = 1
        kind[b, SLOTS - ends[b] : SLOTS] = 2
        target[b, : begin[b]] = NAMED + np.arange(begin[b])
        target[b, SPAN - ends[b] :] = NAMED + np.arange(SLOTS - ends[b], SLOTS)
        places = np.arange(WIDTH)
        own[b] = np.where(kind[b] > 0, NAMED + places, own[b])
    columns = np.full((2, WIDTH, LANES), -5.0, np.float32)
    columns[0, :, :BLOCKS] = own.T
    columns[1, WIDTH - SLOTS :, :BLOCKS] = own.T[:SLOTS]
    return fixed.astype(np.int32), kind, target.astype(np.int32), columns


def frequencies(g_index):
    fixed, kind, target, _ = layout()
    g = g_index.reshape(BLOCKS, SPAN)
    half = GRID // 2
    i, j, k = g // (GRID * GRID), g // GRID % GRID, g % GRID
    i, j, k = [jnp.where(n < half, n, n - GRID) for n in (i, j, k)]
    front = (i > 0) | ((i == 0) & ((j > 0) | ((j == 0) & (k >= 0))))
    sign = jnp.where(front, 1, -1)
    ids = frequency_id(i * sign, j * sign, k * sign)
    first = ids[:, :WIDTH]
    last = jnp.pad(ids[:, SPAN - SLOTS :], ((0, 0), (0, WIDTH - SLOTS)))
    places = jnp.where(kind == 1, first, jnp.where(kind == 2, last, fixed))
    names = jnp.where(target >= 0, target, ids)
    return places, names.astype(jnp.float32), sign.astype(jnp.float32)


def pairs(psi, cond, owner, val_energy, cond_energy, places):
    first, second, third = [jnp.asarray(table) for table in (tables())]
    vm = pl.BlockSpec(memory_space=pltpu.VMEM)
    return pl.pallas_call(
        dft_kernel,
        out_shape=jax.ShapeDtypeStruct((ELEMS, LANES), jnp.bfloat16),
        in_specs=[pl.BlockSpec(memory_space=pltpu.SMEM)] * 3 + [vm] * 7,
        out_specs=vm,
        scratch_shapes=[
            pltpu.VMEM((STEPS, PAD_ROWS, LANES), jnp.float32),
            pltpu.VMEM((STEPS, 2 * WIDE, 41 * LANES), jnp.float32),
            pltpu.VMEM((GRID * 32, LANES), jnp.float32),
            pltpu.VMEM(((REACH + 1) * BACK, STEPS * LANES), jnp.float32),
            pltpu.VMEM((ELEMS, LANES), jnp.float32),
        ],
        compiler_params=pltpu.CompilerParams(vmem_limit_bytes=48 * 2**20),
    )(owner, val_energy, cond_energy, *psi, cond, first, second, third, places)


def sums_kernel(partner, elems, names, signs, columns, out):
    f32, bf = jnp.float32, jnp.bfloat16
    z, yl = lax.axis_index("z"), lax.axis_index("yl")
    m = (lax.axis_index("x") * 2 + lax.axis_index("yh")) * 2 + lax.axis_index("c")
    yl = 1 - yl if partner else yl
    half = SPAN // 2

    def spread(block, side):
        name, sign = names[pl.ds(block, 1), :], signs[pl.ds(block, 1), :]
        if side is not None:
            name, sign = [jnp.where(side == 0, x[:, :half], x[:, half:]) for x in (name, sign)]
        chosen = lax.broadcasted_iota(jnp.int32, (WIDTH, LANES), 1) == block
        place = [jnp.sum(jnp.where(chosen, columns[p], 0.0), 1, keepdims=True) for p in range(2)]
        real = jnp.where(place[0] == name, 1.0, 0.0).astype(bf)
        return real, jnp.where(place[1] == name, sign, 0.0).astype(bf)

    def lanes(n):
        return elems[:, n * 32 : (n + 1) * 32, :].reshape(-1, LANES)

    def widened(tiles, hot):
        real = jnp.dot(jnp.concatenate(tiles[:3], 1), hot[0], preferred_element_type=f32)
        imag = jnp.dot(jnp.concatenate(tiles[2:], 1), hot[1], preferred_element_type=f32)
        return real.astype(bf), imag.astype(bf)

    left = widened([lanes(BOTH + n) for n in range(BOTH)], spread(z, yl))
    right = widened([lanes(n) for n in range(BOTH)], spread(m, None))
    over = (((0,), (0,)), ((), ()))
    total = lax.dot_general(left[0], right[0], over, preferred_element_type=f32)
    total += lax.dot_general(left[1], right[1], over, preferred_element_type=f32)
    out[...] = (total * (-1.0 / math.sqrt(STEPS * 512))).astype(out.dtype)


def sums(elems, names, signs, partner):
    vm = pl.BlockSpec(memory_space=pltpu.VMEM)
    return pl.pallas_call(
        functools.partial(sums_kernel, partner),
        out_shape=jax.ShapeDtypeStruct((SPAN // 2, SPAN), jnp.bfloat16 if partner else jnp.float32),
        in_specs=[vm] * 4,
        out_specs=vm,
        cost_estimate=pl.CostEstimate(flops=10**9, bytes_accessed=2 * 2**20, transcendentals=0),
        compiler_params=pltpu.CompilerParams(vmem_limit_bytes=48 * 2**20),
    )(elems, names, signs, jnp.asarray(layout()[3]))


def body(valence, conduction, val_energy, cond_energy, owner, g_index):
    psi, g_index = from_owners(valence, owner, g_index)
    cond = in_rows(conduction)
    places, names, signs = frequencies(g_index)
    elems = pairs(psi, cond, owner, val_energy, cond_energy, places)

    elems = lax.all_gather(elems, "z", axis=0, tiled=True)
    elems = exchange(turn(elems), COL)
    away = lax.ppermute(sums(elems, names, signs, True), "yl", SWAP)
    return sums(elems, names, signs, False) + away.astype(jnp.float32)


def solution(mesh):
    every = P(AXES)
    return jax.shard_map(
        body,
        mesh=Mesh(mesh.devices.reshape(SIZES), AXES),
        in_specs=(P(AXES, None), P(AXES, None), P(), every, P(), P()),
        out_specs=P(ROW, COL),
        check_vma=False,
    )
```

```python
import math

import jax
import jax.numpy as jnp
import ml_dtypes
import numpy as np
from jax import lax
from jax.experimental import pallas as pl
from jax.experimental.pallas import tpu as pltpu
from jax.sharding import Mesh, PartitionSpec as P

GRID = 72
STEPS = 2
AXES = ("z", "yl", "x", "yh", "c")
SIZES = (16, 2, 4, 2, 2)
ROW = ("z", "yl")
COL = ("x", "yh", "c")
PLANE = ("yl", "x", "yh", "c")
TILE = ("yl", "x", "yh")
QUAD = ("x", "yh")
LANES = 128
PIECE = 6
CHUNK = 16 * PIECE
SWAP = [(0, 1), (1, 0)]
NG = 8192
BLOCKS = 16
SPAN = NG // BLOCKS
SLOTS = 320
WIDTH = 384
BOTH = 2 * SLOTS // LANES
LINES = STEPS * BOTH
ELEMS = LINES * BLOCKS
NAMED = 1 << 20
REACH=12
KEPT=2*REACH+1
HALF=GRID//2
PAIR=GRID*GRID*2//LANES
ROWS=GRID**3//LANES
WIDE=16
BACK=16
SLOT=32
PAD_ROWS=40*PAIR


def exchange(x, axis):
    return lax.all_to_all(x, axis, split_axis=0, concat_axis=0, tiled=True)


def rows_kernel(flat, out, rows):
    done = ROWS // 32 * 32
    for at in range(0, done, 32):
        part = flat[:, at * LANES : (at + 32) * LANES].astype(jnp.float32)
        rows[at : at + 32, :] = part.reshape(32, LANES)
    part = flat[:, done * LANES :].astype(jnp.float32)
    rows[done:ROWS, :] = part.reshape(ROWS - done, LANES)
    rows[ROWS:, :] = jnp.zeros((32 * CHUNK - ROWS, LANES), jnp.float32)
    out[...] = rows[...].astype(jnp.bfloat16)


def in_rows(flat):
    return pl.pallas_call(
        rows_kernel,
        out_shape=jax.ShapeDtypeStruct((32 * CHUNK, LANES), jnp.bfloat16),
        in_specs=[pl.BlockSpec(memory_space=pltpu.VMEM)],
        out_specs=pl.BlockSpec(memory_space=pltpu.VMEM),
        scratch_shapes=[pltpu.VMEM((32 * CHUNK, LANES), jnp.float32)],
        cost_estimate=pl.CostEstimate(flops=0, bytes_accessed=4 * 2**20, transcendentals=0),
        compiler_params=pltpu.CompilerParams(vmem_limit_bytes=32 * 2**20),
    )(flat)


def from_owners(shard, owner, late):
    parts = exchange(in_rows(shard).reshape(32, CHUNK, LANES), PLANE)
    parts = [lax.dynamic_index_in_dim(parts, owner[s] & 31, 0, False) for s in range(STEPS)]
    parts = lax.all_gather(jnp.concatenate(parts, axis=0), "z", axis=0, tiled=True)
    parts = parts.reshape(16, STEPS, CHUNK, LANES)
    parts = [lax.dynamic_index_in_dim(parts[:, s], owner[s] >> 5, 0, False) for s in range(STEPS)]
    parts = jnp.concatenate(parts, axis=0)
    parts = exchange(jnp.broadcast_to(parts[None], (16,) + parts.shape), TILE)
    parts, *late = lax.optimization_barrier((parts, *late))
    return (parts, lax.ppermute(parts, "c", SWAP)), late


def split(x):
    high=x.astype(jnp.bfloat16)
    return high,(x-high.astype(jnp.float32)).astype(jnp.bfloat16)

def split_np(x):
    h=x.astype(ml_dtypes.bfloat16)
    return h,(x-h.astype(np.float64)).astype(ml_dtypes.bfloat16)

def tables():
    point=np.arange(GRID)
    def cs(freq):
        ang=2*math.pi*((freq[:,None]*point[None,:])%GRID)/GRID
        return np.cos(ang),np.sin(ang)
    c,s=cs(np.arange(REACH+1))
    t=np.zeros((2,WIDE,2,40))
    t[0,:REACH+1,0,:HALF]=c[:,0::2]; t[0,:REACH+1,1,:HALF]=c[:,1::2]
    t[1,:REACH+1,0,:HALF]=-s[:,0::2]; t[1,:REACH+1,1,:HALF]=-s[:,1::2]
    t=t.reshape(2*WIDE,80)
    h,l=split_np(t)
    first=np.concatenate([h,h,l],1)
    c,s=cs(np.arange(-REACH,REACH+1))
    w=np.zeros((2,LANES,4,SLOT))
    w[0,:GRID,0,:KEPT]=c.T; w[0,:GRID,1,:KEPT]=-s.T
    w[1,:GRID,0,:KEPT]=s.T; w[1,:GRID,1,:KEPT]=c.T
    w[:,:,2]=w[:,:,1]; w[:,:,3]=-w[:,:,0]
    w=w.reshape(2*LANES,LANES)
    h,l=split_np(w)
    third=np.concatenate([h,l],1)
    u=np.zeros((2,2,BACK,GRID))
    u[0,0,:REACH+1]=c[0::2]; u[0,1,:REACH]=c[1::2]
    u[1,0,:REACH+1]=s[0::2]; u[1,1,:REACH]=s[1::2]
    u=u.reshape(4*BACK,GRID)
    h,l=split_np(u)
    second=np.concatenate([h,h,l],1)
    return first,second,third

def dft_kernel(owner, val_energy, cond_energy, same, other, cond, first, second, third, places, out, vals, held, mixed, spread, lined):
    f32=jnp.float32; bf=jnp.bfloat16
    core = lax.axis_index("c")
    for s in range(STEPS):
        vals[s, 32 * CHUNK :, :] = jnp.zeros((PAD_ROWS - 32 * CHUNK, LANES), f32)
        for t in range(16):
            for psi, side in ((same, core), (other, 1 - core)):
                here = pl.ds(pl.multiple_of((2 * t + side) * CHUNK, CHUNK), CHUNK)
                band = psi[t, s * CHUNK : (s + 1) * CHUNK, :].astype(f32)
                vals[s, here, :] = band * cond[here, :].astype(f32)
    left=lax.broadcasted_iota(jnp.int32,(40,LANES),1)<LANES//2
    table=first[...]
    zero=jnp.zeros((40,LANES),f32)
    rolled=[pltpu.roll(vals[s,pl.ds(40,40,stride=PAIR),:],LANES//2,1) for s in range(STEPS)]
    for t in range(41):
        cols=[]
        for s in range(STEPS):
            even=vals[s,pl.ds(t,40,stride=PAIR),:]
            here=rolled[s]
            ahead=pltpu.roll(vals[s,pl.ds(41+t,40,stride=PAIR),:],LANES//2,1) if t<40 else zero
            rolled[s]=ahead
            odd=jnp.where(left,here,ahead)
            x=jnp.concatenate([even,odd],0)
            h=x.astype(bf).astype(f32)
            cols.append(jnp.concatenate([h,x-h,h],0).astype(bf))
        y=jnp.dot(table,jnp.concatenate(cols,1),preferred_element_type=f32)
        for s in range(STEPS):
            held[s,:,t*LANES:(t+1)*LANES]=y[:,s*LANES:(s+1)*LANES]
    w=third[...]
    group=GRID
    for j0 in range(0,GRID,group):
        parts=[[],[]]
        for j in range(j0,j0+group):
            for s in range(STEPS):
                x=held[s,:,j*GRID:j*GRID+LANES]
                parts[0].append(x[:WIDE]); parts[1].append(x[WIDE:])
        x=jnp.concatenate([jnp.concatenate(parts[0],0),jnp.concatenate(parts[1],0)],1)
        h,l=split(x)
        y=jnp.dot(h,w,preferred_element_type=f32)
        z=jnp.dot(l,w[:,:LANES],preferred_element_type=f32)
        mixed[j0*32:(j0+group)*32,:]=y[:,:LANES]+y[:,LANES:]+z
    table=second[...]
    near = lax.broadcasted_iota(jnp.int32, (BACK, LANES), 1) < LANES // 2
    factors = []
    for s in range(STEPS):
        gap = jnp.full((BACK, LANES), cond_energy[0] - val_energy[owner[s]], f32)
        factors.append(jnp.sqrt(4.0 / gap) / math.sqrt(GRID**3))
    for i in range(REACH+1):
        cols=[]
        for s in range(STEPS):
            x=mixed[pl.ds(s*WIDE+i,GRID,stride=32),:]
            h=x.astype(bf).astype(f32)
            cols.append(jnp.concatenate([h,x-h,h],0).astype(bf))
        y=jnp.dot(table,jnp.concatenate(cols,1),preferred_element_type=f32)
        for s in range(STEPS):
            z=y[:,s*LANES:(s+1)*LANES]
            r=z[:2*BACK]+pltpu.roll(z[2*BACK:],LANES//2,1)
            r=jnp.where(near,r[:BACK],pltpu.roll(r[BACK:],LANES//2,1))*factors[s]
            spread[i*BACK:(i+1)*BACK, s*LANES:(s+1)*LANES]=r
    rows = (REACH + 1) * BACK
    data = spread[...].T.astype(bf)
    at = lax.broadcasted_iota(jnp.int32, (rows, WIDTH), 0)
    slot = lax.broadcasted_iota(jnp.int32, (SLOT, WIDTH), 0)
    gap = jnp.zeros((STEPS, 2 * LANES), f32)
    for b in range(BLOCKS):
        place = places[b : b + 1, :]
        hot = jnp.where(at == (place >> 7), 1.0, 0.0).astype(bf)
        y = jnp.dot(data, hot, preferred_element_type=f32)
        keep = slot == (place & (SLOT - 1))
        even = (place & (LANES // 2)) == 0
        got = []
        for s in range(STEPS):
            half = y[s * LANES : (s + 1) * LANES]
            half = jnp.where(even, half[: LANES // 2], half[LANES // 2 :])
            for part in (half[:SLOT], half[SLOT:]):
                got.append(jnp.sum(jnp.where(keep, part, 0.0), 0, keepdims=True))
        real = jnp.concatenate([jnp.concatenate(got[0::2], 0), gap], 1)
        imag = pltpu.roll(jnp.concatenate(got[1::2], 0), WIDTH - SLOTS, 1)
        both = real + jnp.concatenate([gap, imag], 1)
        for s in range(STEPS):
            for n in range(BOTH):
                at_line = (s * BOTH + n) * BLOCKS + b
                lined[at_line : at_line + 1, :] = both[s : s + 1, n * LANES : (n + 1) * LANES]
    out[...] = lined[...].astype(bf)


def turn_kernel(gathered, out, rows):
    rows[...] = gathered[...].astype(jnp.float32)
    for b in range(BLOCKS):
        for line in range(LINES):
            s, n = line // BOTH, line % BOTH
            got = rows[pl.ds(line * BLOCKS + b, 16, stride=ELEMS), :]
            to = (n * STEPS + s) * 16
            out[b, to : to + 16, :] = got.astype(jnp.bfloat16)
    chosen = out[lax.axis_index("z"), :ELEMS, :]
    for b in range(BLOCKS):
        out[b, ELEMS:, :] = chosen


def turn(gathered):
    vm = pl.BlockSpec(memory_space=pltpu.VMEM)
    return pl.pallas_call(
        turn_kernel,
        out_shape=jax.ShapeDtypeStruct((BLOCKS, 2 * ELEMS, LANES), jnp.bfloat16),
        in_specs=[vm],
        out_specs=vm,
        scratch_shapes=[pltpu.VMEM((16 * ELEMS, LANES), jnp.float32)],
        compiler_params=pltpu.CompilerParams(vmem_limit_bytes=32 * 2**20),
    )(gathered)


def frequency_id(i, j, k):
    j = j + REACH
    return (i * BACK + (j >> 1)) * LANES + (j & 1) * (LANES // 2) + k + REACH


def layout():
    axis = np.arange(-REACH, REACH + 1)
    grid = np.stack(np.meshgrid(axis, axis, axis, indexing="ij"), -1).reshape(-1, 3)
    length = (grid**2).sum(1)
    fixed = np.full((BLOCKS, WIDTH), -1)
    kind = np.zeros((BLOCKS, WIDTH), np.int32)
    target = np.full((BLOCKS, SPAN), -1)
    own = np.full((BLOCKS, WIDTH), -5)
    begin = [0] * BLOCKS
    shells = [[] for _ in range(BLOCKS)]
    ends = [0] * BLOCKS
    at = 0
    for value in np.unique(length):
        if at >= NG:
            break
        shell = grid[length == value]
        stop = min(at + len(shell), NG)
        for b in range(at // SPAN, (stop - 1) // SPAN + 1):
            low, high = max(at, b * SPAN), min(stop, b * SPAN + SPAN)
            if high - low == len(shell) or 2 * (high - low) > len(shell):
                i, j, k = shell.T
                front = (i > 0) | ((i == 0) & ((j > 0) | ((j == 0) & (k >= 0))))
                i, j, k = shell[front].T
                shells[b].append(frequency_id(i, j, k))
            elif low == b * SPAN:
                begin[b] = high - low
            else:
                assert high == b * SPAN + SPAN
                ends[b] = high - low
        at = stop
    for b in range(BLOCKS):
        known = np.concatenate(shells[b])
        assert begin[b] + len(known) + ends[b] <= SLOTS
        fixed[b, begin[b] : begin[b] + len(known)] = known
        own[b, begin[b] : begin[b] + len(known)] = known
        kind[b, : begin[b]] = 1
        kind[b, SLOTS - ends[b] : SLOTS] = 2
        target[b, : begin[b]] = NAMED + np.arange(begin[b])
        target[b, SPAN - ends[b] :] = NAMED + np.arange(SLOTS - ends[b], SLOTS)
        places = np.arange(WIDTH)
        own[b] = np.where(kind[b] > 0, NAMED + places, own[b])
    columns = np.full((2, WIDTH, LANES), -5.0, np.float32)
    columns[0, :, :BLOCKS] = own.T
    columns[1, WIDTH - SLOTS :, :BLOCKS] = own.T[:SLOTS]
    return fixed.astype(np.int32), kind, target.astype(np.int32), columns


def frequencies(g_index):
    fixed, kind, target, _ = layout()
    g = g_index.reshape(BLOCKS, SPAN)
    half = GRID // 2
    i, j, k = g // (GRID * GRID), g // GRID % GRID, g % GRID
    i, j, k = [jnp.where(n < half, n, n - GRID) for n in (i, j, k)]
    front = (i > 0) | ((i == 0) & ((j > 0) | ((j == 0) & (k >= 0))))
    sign = jnp.where(front, 1, -1)
    ids = frequency_id(i * sign, j * sign, k * sign)
    first = ids[:, :WIDTH]
    last = jnp.pad(ids[:, SPAN - SLOTS :], ((0, 0), (0, WIDTH - SLOTS)))
    places = jnp.where(kind == 1, first, jnp.where(kind == 2, last, fixed))
    names = jnp.where(target >= 0, target, ids)
    return places, names.astype(jnp.float32), sign.astype(jnp.float32)


def pairs(psi, cond, owner, val_energy, cond_energy, places):
    first, second, third = [jnp.asarray(table) for table in (tables())]
    vm = pl.BlockSpec(memory_space=pltpu.VMEM)
    return pl.pallas_call(
        dft_kernel,
        out_shape=jax.ShapeDtypeStruct((ELEMS, LANES), jnp.bfloat16),
        in_specs=[pl.BlockSpec(memory_space=pltpu.SMEM)] * 3 + [vm] * 7,
        out_specs=vm,
        scratch_shapes=[
            pltpu.VMEM((STEPS, PAD_ROWS, LANES), jnp.float32),
            pltpu.VMEM((STEPS, 2 * WIDE, 41 * LANES), jnp.float32),
            pltpu.VMEM((GRID * 32, LANES), jnp.float32),
            pltpu.VMEM(((REACH + 1) * BACK, STEPS * LANES), jnp.float32),
            pltpu.VMEM((ELEMS, LANES), jnp.float32),
        ],
        compiler_params=pltpu.CompilerParams(vmem_limit_bytes=48 * 2**20),
    )(owner, val_energy, cond_energy, *psi, cond, first, second, third, places)


def spreads_kernel(names, signs, columns, *outs):
    bf = jnp.bfloat16
    z, yl = lax.axis_index("z"), lax.axis_index("yl")
    m = (lax.axis_index("x") * 2 + lax.axis_index("yh")) * 2 + lax.axis_index("c")
    half = SPAN // 2

    def spread(block, side):
        name, sign = names[pl.ds(block, 1), :], signs[pl.ds(block, 1), :]
        if side is not None:
            name, sign = [jnp.where(side == 0, x[:, :half], x[:, half:]) for x in (name, sign)]
        chosen = lax.broadcasted_iota(jnp.int32, (WIDTH, LANES), 1) == block
        place = [jnp.sum(jnp.where(chosen, columns[p], 0.0), 1, keepdims=True) for p in range(2)]
        real = jnp.where(place[0] == name, 1.0, 0.0).astype(bf)
        return real, jnp.where(place[1] == name, sign, 0.0).astype(bf)

    made = spread(m, None) + spread(z, 1 - yl) + spread(z, yl)
    for out, hot in zip(outs, made):
        out[...] = hot


def spreads(names, signs):
    vm = pl.BlockSpec(memory_space=pltpu.VMEM)
    widths = [SPAN] * 2 + [SPAN // 2] * 4
    return pl.pallas_call(
        spreads_kernel,
        out_shape=[jax.ShapeDtypeStruct((WIDTH, n), jnp.bfloat16) for n in widths],
        in_specs=[vm] * 3,
        out_specs=[vm] * 6,
        compiler_params=pltpu.CompilerParams(vmem_limit_bytes=32 * 2**20),
    )(names, signs, jnp.asarray(layout()[3]))


def sums_kernel(elems, col_re, col_im, row_re, row_im, out):
    f32, bf = jnp.float32, jnp.bfloat16

    def lanes(n):
        return elems[:, n * 32 : (n + 1) * 32, :].reshape(-1, LANES)

    def widened(tiles, hot):
        real = jnp.dot(jnp.concatenate(tiles[:3], 1), hot[0][...], preferred_element_type=f32)
        imag = jnp.dot(jnp.concatenate(tiles[2:], 1), hot[1][...], preferred_element_type=f32)
        return real.astype(bf), imag.astype(bf)

    left = widened([lanes(BOTH + n) for n in range(BOTH)], (row_re, row_im))
    right = widened([lanes(n) for n in range(BOTH)], (col_re, col_im))
    over = (((0,), (0,)), ((), ()))
    total = lax.dot_general(left[0], right[0], over, preferred_element_type=f32)
    total += lax.dot_general(left[1], right[1], over, preferred_element_type=f32)
    out[...] = (total * (-1.0 / math.sqrt(STEPS * 512))).astype(out.dtype)


def sums(elems, cols, rows, dtype):
    vm = pl.BlockSpec(memory_space=pltpu.VMEM)
    return pl.pallas_call(
        sums_kernel,
        out_shape=jax.ShapeDtypeStruct((SPAN // 2, SPAN), dtype),
        in_specs=[vm] * 5,
        out_specs=vm,
        cost_estimate=pl.CostEstimate(flops=10**9, bytes_accessed=2 * 2**20, transcendentals=0),
        compiler_params=pltpu.CompilerParams(vmem_limit_bytes=48 * 2**20),
    )(elems, *cols, *rows)


def body(valence, conduction, val_energy, cond_energy, owner, g_index):
    places, names, signs = frequencies(g_index)
    psi, (places, *hot) = from_owners(valence, owner, (places, *spreads(names, signs)))
    cond = in_rows(conduction)
    elems = pairs(psi, cond, owner, val_energy, cond_energy, places)

    elems = lax.all_gather(elems, "z", axis=0, tiled=True)
    elems = exchange(turn(elems), COL)
    away = lax.ppermute(sums(elems, hot[:2], hot[2:4], jnp.bfloat16), "yl", SWAP)
    return sums(elems, hot[:2], hot[4:], jnp.float32) + away.astype(jnp.float32)


def solution(mesh):
    every = P(AXES)
    return jax.shard_map(
        body,
        mesh=Mesh(mesh.devices.reshape(SIZES), AXES),
        in_specs=(P(AXES, None), P(AXES, None), P(), every, P(), P()),
        out_specs=P(ROW, COL),
        check_vma=False,
    )
```
